32 devices in a mesh: grp: 2 (over y), space: 4 (over z), tm: 2 (over x), sub: 2 (over core).
Axes of the slice: x: 2, y: 2, z: 4, core: 2. Of those that a mesh axis runs over, the one named last changes fastest.
Arguments:
- gauge_links: float32 [4, 18, 8, 16, 4, 128], P(None, None, ('grp', 'tm'), 'space', 'sub'), parts along dimension 2, may hold values from -1 to 1, as said below
- active_blocks: int32 [4, 4, 2, 4, 4], P('grp'), parts along dimension 0, may hold values from 0 to 1, as said below
- conv_in: bfloat16 [2, 81, 12, 64], replicated, may hold values from -0.1875 to 0.1875
- bias_in: float32 [2, 64], replicated, may hold values from -3 to 3
- conv_out: bfloat16 [2, 64, 24], replicated, may hold values from -0.75 to 0.75
- bias_out: float32 [2, 24], replicated, may hold values from -3 to 3
Outputs:
- flowed_links: float32 [4, 18, 8, 16, 4, 128], P(None, None, ('grp', 'tm'), 'space', 'sub'), parts along dimension 2
The draws below stay inside these ranges and needn't reach their ends.
There are 2 independent parts, one for each index of `grp`. The reference program is written for one: setup_inputs(seed, part) draws one part's arguments, and reference() takes and returns one part's arrays. A program takes and returns all parts, laid end to end along the dimension named above; an argument that names none is the same for every part. Nothing has to cross between parts.
Inputs may be any that keep to these rules, and one draw needn't show every extreme that they name: For every direction and site the 3x3 complex matrix of gauge_links is unitary. `active_blocks`: for each layer and direction the active blocks form a checkerboard over time, x and y blocks; which of its two colours is active is drawn for each layer and direction.
All inputs are finite; a program needn't handle non-finite values.
Results may differ from the reference program's by a relative error of at most 0.0019.
Values may be sent and summed in bfloat16 or wider, within the bound.
No kernel may reach another device: no remote copies, remote signals or barrier semaphores. Data moves between devices by JAX's collectives and lax.ppermute only.
A program may use at most 128 MiB of HBM per device.

```python
import jax
import jax.numpy as jnp
from jax import lax

TT = 2
XL = 4
YL = 2
NZ = 128
LAYERS = 2
HID = 64
CIN = 12
TAPS = 81
NCOEF = 24
NT = 4
NX = 16
NY = 4
NBY = 4
N_SPACE = 4
N_TM = 2


def multiply_drawn(left, right):
    left_re, left_im = left
    right_re, right_im = right
    real_part = jnp.sum(left_re[:, :, None] * right_re[None] - left_im[:, :, None] * right_im[None], axis=1)
    imag_part = jnp.sum(left_re[:, :, None] * right_im[None] + left_im[:, :, None] * right_re[None], axis=1)
    return (real_part, imag_part)


def scalar_mul_drawn(left, right):
    return (left[0] * right[0] - left[1] * right[1], left[0] * right[1] + left[1] * right[0])


def cayley_drawn(generator):
    gen_re, gen_im = generator
    identity = jnp.eye(3, dtype=jnp.float32).reshape((3, 3) + (1,) * (gen_re.ndim - 2))
    lower_re = identity - 0.5 * gen_re
    lower_im = -0.5 * gen_im
    upper = (identity + 0.5 * gen_re, 0.5 * gen_im)

    def element(i, j):
        return (lower_re[i, j], lower_im[i, j])
    adj_rows_re = []
    adj_rows_im = []
    for i in range(3):
        row_re = []
        row_im = []
        for j in range(3):
            first_term = scalar_mul_drawn(element((j + 1) % 3, (i + 1) % 3), element((j + 2) % 3, (i + 2) % 3))
            second_term = scalar_mul_drawn(element((j + 1) % 3, (i + 2) % 3), element((j + 2) % 3, (i + 1) % 3))
            row_re.append(first_term[0] - second_term[0])
            row_im.append(first_term[1] - second_term[1])
        adj_rows_re.append(jnp.stack(row_re))
        adj_rows_im.append(jnp.stack(row_im))
    adj_re = jnp.stack(adj_rows_re)
    adj_im = jnp.stack(adj_rows_im)
    det_re = jnp.zeros_like(gen_re[0, 0])
    det_im = jnp.zeros_like(gen_re[0, 0])
    for k in range(3):
        product = scalar_mul_drawn(element(0, k), (adj_re[k, 0], adj_im[k, 0]))
        det_re = det_re + product[0]
        det_im = det_im + product[1]
    det_norm = det_re * det_re + det_im * det_im
    scale_re = det_re / det_norm
    scale_im = -det_im / det_norm
    numerator = multiply_drawn((adj_re, adj_im), upper)
    return (numerator[0] * scale_re - numerator[1] * scale_im, numerator[0] * scale_im + numerator[1] * scale_re)


def draw_gauge_links(key, part):

    def one_direction(direction):
        subkey = jax.random.fold_in(key, direction)
        sampled = 1.2 * jax.random.normal(subkey, (2, 3, 3, NT, NX, NY, NZ), jnp.float32)
        generator = (0.5 * (sampled[0] - jnp.swapaxes(sampled[0], 0, 1)), 0.5 * (sampled[1] + jnp.swapaxes(sampled[1], 0, 1)))
        rotation = cayley_drawn(generator)
        return jnp.stack(rotation).reshape((18, NT, NX, NY, NZ))
    return lax.map(one_direction, jnp.arange(4))


def draw_active_blocks(key, part):
    parity = jax.random.randint(jax.random.fold_in(key, 7), (LAYERS, 4, 1, 1, 1), 0, 2)
    time_block = jnp.arange(N_TM, dtype=jnp.int32)[:, None, None]
    x_block = jnp.arange(N_SPACE, dtype=jnp.int32)[None, :, None]
    y_block = jnp.arange(NBY, dtype=jnp.int32)[None, None, :]
    pattern = (time_block + x_block + y_block)[None, None]
    return ((pattern + parity) % 2).astype(jnp.int32)


def centred(rng, dims, deviation, reach, kind=jnp.bfloat16):
    return jnp.clip(deviation * jax.random.normal(rng, dims, jnp.float32), -reach, reach).astype(kind)


def setup_inputs(seed: int = 0, part: int = 0) -> dict:
    seeds = jax.random.split(jax.random.key(seed), 7)
    own_keys = jax.random.split(jax.random.fold_in(seeds[6], part), 7)
    gauge_links = draw_gauge_links(jax.random.fold_in(jax.random.fold_in(seeds[6], part), 71), part)
    active_blocks = draw_active_blocks(jax.random.fold_in(jax.random.fold_in(seeds[6], part), 71), part)
    conv_in = centred(seeds[2], (LAYERS, TAPS, CIN, HID), (TAPS * CIN) ** -0.5, 0.1875)
    bias_in = centred(seeds[3], (LAYERS, HID), 0.5, 3.0, jnp.float32)
    conv_out = centred(seeds[4], (LAYERS, HID, NCOEF), HID ** -0.5, 0.75)
    bias_out = centred(seeds[5], (LAYERS, NCOEF), 0.5, 3.0, jnp.float32)
    return dict(gauge_links=gauge_links, active_blocks=active_blocks, conv_in=conv_in, bias_in=bias_in, conv_out=conv_out, bias_out=bias_out)


PAIRS = ((0, 1), (0, 2), (0, 3), (1, 2), (1, 3), (2, 3))


def unit_step(direction, sign):
    return tuple(sign if d == direction else 0 for d in range(4))


def offset_sum(first_off, second_off):
    return tuple(a + b for a, b in zip(first_off, second_off))


def multiply(left, right):
    left_re, left_im = left
    right_re, right_im = right
    real_part = jnp.sum(left_re[:, :, None] * right_re[None] - left_im[:, :, None] * right_im[None], axis=1)
    imag_part = jnp.sum(left_re[:, :, None] * right_im[None] + left_im[:, :, None] * right_re[None], axis=1)
    return (real_part, imag_part)


def dagger(matrix):
    return (jnp.swapaxes(matrix[0], 0, 1), -jnp.swapaxes(matrix[1], 0, 1))


def scalar_mul(left, right):
    return (left[0] * right[0] - left[1] * right[1], left[0] * right[1] + left[1] * right[0])


def cayley(generator):
    gen_re, gen_im = generator
    identity = jnp.eye(3, dtype=jnp.float32).reshape((3, 3) + (1,) * (gen_re.ndim - 2))
    lower_re = identity - 0.5 * gen_re
    lower_im = -0.5 * gen_im
    upper = (identity + 0.5 * gen_re, 0.5 * gen_im)

    def element(i, j):
        return (lower_re[i, j], lower_im[i, j])

    adj_rows_re = []
    adj_rows_im = []
    for i in range(3):
        row_re = []
        row_im = []
        for j in range(3):
            first_term = scalar_mul(element((j + 1) % 3, (i + 1) % 3), element((j + 2) % 3, (i + 2) % 3))
            second_term = scalar_mul(element((j + 1) % 3, (i + 2) % 3), element((j + 2) % 3, (i + 1) % 3))
            row_re.append(first_term[0] - second_term[0])
            row_im.append(first_term[1] - second_term[1])
        adj_rows_re.append(jnp.stack(row_re))
        adj_rows_im.append(jnp.stack(row_im))
    adj_re = jnp.stack(adj_rows_re)
    adj_im = jnp.stack(adj_rows_im)
    det_re = jnp.zeros_like(gen_re[0, 0])
    det_im = jnp.zeros_like(gen_re[0, 0])
    for k in range(3):
        product = scalar_mul(element(0, k), (adj_re[k, 0], adj_im[k, 0]))
        det_re = det_re + product[0]
        det_im = det_im + product[1]
    det_norm = det_re * det_re + det_im * det_im
    scale_re = det_re / det_norm
    scale_im = -det_im / det_norm
    numerator = multiply((adj_re, adj_im), upper)
    return (numerator[0] * scale_re - numerator[1] * scale_im, numerator[0] * scale_im + numerator[1] * scale_re)


def antiherm(matrix):
    real_part, imag_part = matrix
    trace_im = imag_part[0, 0] + imag_part[1, 1] + imag_part[2, 2]
    identity = jnp.eye(3, dtype=jnp.float32).reshape((3, 3) + (1,) * (real_part.ndim - 2))
    return (0.5 * (real_part - jnp.swapaxes(real_part, 0, 1)),
            0.5 * (imag_part + jnp.swapaxes(imag_part, 0, 1)) - identity * (trace_im / 3.0))


def loop_up(lookup, major, minor):
    zero = (0, 0, 0, 0)
    step_major = unit_step(major, 1)
    step_minor = unit_step(minor, 1)
    value = multiply(lookup(major, zero), lookup(minor, step_major))
    value = multiply(value, dagger(lookup(major, step_minor)))
    return multiply(value, dagger(lookup(minor, zero)))


def loop_down(lookup, major, minor):
    zero = (0, 0, 0, 0)
    back_minor = unit_step(minor, -1)
    corner = offset_sum(unit_step(major, 1), back_minor)
    value = multiply(lookup(major, zero), dagger(lookup(minor, corner)))
    value = multiply(value, dagger(lookup(major, back_minor)))
    return multiply(value, lookup(minor, back_minor))


def features(lookup):
    channels = []
    for major, minor in PAIRS:
        plaquette = loop_up(lookup, major, minor)
        channels.append((plaquette[0][0, 0] + plaquette[0][1, 1] + plaquette[0][2, 2]) / 3.0)
        channels.append((plaquette[1][0, 0] + plaquette[1][1, 1] + plaquette[1][2, 2]) / 3.0)
    return jnp.stack(channels)


def update(lookup, weights_loop, major):
    summed_re = jnp.float32(0.0)
    summed_im = jnp.float32(0.0)
    others = [minor for minor in range(4) if minor != major]
    for j, minor in enumerate(others):
        upper_loop = loop_up(lookup, major, minor)
        lower_loop = loop_down(lookup, major, minor)
        weight_up = weights_loop[6 * major + 2 * j]
        weight_down = weights_loop[6 * major + 2 * j + 1]
        summed_re = summed_re + weight_up * upper_loop[0] + weight_down * lower_loop[0]
        summed_im = summed_im + weight_up * upper_loop[1] + weight_down * lower_loop[1]
    rotation = cayley(antiherm((summed_re, summed_im)))
    return multiply(rotation, lookup(major, (0, 0, 0, 0)))


def convolve(traces, kernel_all):
    kernel = kernel_all.reshape(9, -1, kernel_all.shape[-1])
    site_count = traces.shape[1] * traces.shape[2] * traces.shape[3] * traces.shape[4]
    summed = jnp.zeros((kernel.shape[-1], site_count), jnp.float32)
    for a in range(3):
        for b in range(3):
            pieces = [jnp.roll(traces, (1 - a, 1 - b, 1 - c, 1 - d), axis=(1, 2, 3, 4))
                      for c in range(3) for d in range(3)]
            patches = jnp.concatenate(pieces, axis=0).reshape(kernel.shape[1], site_count)
            summed = summed + jnp.dot(kernel[a * 3 + b].T, patches, preferred_element_type=jnp.float32)
    return summed


def roll_lookup(field):
    extent = field.shape[2:]

    def lookup(direction, offset):
        window = jnp.roll(field[direction], tuple(-o for o in offset), axis=(1, 2, 3, 4))
        matrix = window.reshape((2, 3, 3) + extent)
        return (matrix[0], matrix[1])
    return lookup


def coupling(lattice, active_blocks, conv_in, bias_in, conv_out, bias_out, level):
    extent = lattice.shape[2:]
    masks = []
    for major in range(4):
        blocks_on = active_blocks[level, major]
        blocks_on = jnp.repeat(jnp.repeat(jnp.repeat(blocks_on, TT, axis=0), XL, axis=1), YL // 2, axis=2)
        masks.append(blocks_on > 0)
    active_all = jnp.stack(masks)
    frozen = jnp.where(active_all[:, None, :, :, :, None], jnp.zeros_like(lattice), lattice)
    lookup = roll_lookup(lattice)
    traces = features(roll_lookup(frozen)).astype(jnp.bfloat16)
    hidden = convolve(traces, conv_in[level])
    hidden_act = jnp.tanh(hidden + bias_in[level][:, None]).astype(jnp.bfloat16)
    weights_loop = (jnp.dot(conv_out[level].T, hidden_act, preferred_element_type=jnp.float32)
                    + bias_out[level][:, None]).reshape((-1,) + extent)
    results = []
    for major in range(4):
        current = lookup(major, (0, 0, 0, 0))
        turned = update(lookup, weights_loop, major)
        active = active_all[major][:, :, :, None]
        real_part = jnp.where(active, turned[0], current[0])
        imag_part = jnp.where(active, turned[1], current[1])
        results.append(jnp.stack([real_part, imag_part]).reshape((18,) + extent))
    return jnp.stack(results)


def reference(gauge_links, active_blocks, conv_in, bias_in, conv_out, bias_out):
    after_one = coupling(gauge_links, active_blocks, conv_in, bias_in, conv_out, bias_out, 0)
    shifted = jnp.roll(after_one, -(XL // 2), axis=3)
    return coupling(shifted, active_blocks, conv_in, bias_in, conv_out, bias_out, 1)
```

```python
import jax
import jax.numpy as jnp
from jax import lax
from jax.experimental import pallas as pl
from jax.experimental.pallas import tpu as pltpu
from jax.sharding import PartitionSpec as P

PAIRS = ((0, 1), (0, 2), (0, 3), (1, 2), (1, 3), (2, 3))
F32 = jnp.float32
BF16 = jnp.bfloat16
BASE = 8
LIMIT = 56 * 1024 * 1024


def mm(a, b, a_dag=False, b_dag=False):
    out_re, out_im = [], []
    for i in range(3):
        row_re, row_im = [], []
        for j in range(3):
            re = im = None
            for k in range(3):
                ar, ai = (a[0][k][i], a[1][k][i]) if a_dag else (a[0][i][k], a[1][i][k])
                br, bi = (b[0][j][k], b[1][j][k]) if b_dag else (b[0][k][j], b[1][k][j])
                if a_dag:
                    r, m = ar * br + ai * bi, ar * bi - ai * br
                elif b_dag:
                    r, m = ar * br + ai * bi, ai * br - ar * bi
                else:
                    r, m = ar * br - ai * bi, ar * bi + ai * br
                re = r if re is None else re + r
                im = m if im is None else im + m
            row_re.append(re)
            row_im.append(im)
        out_re.append(row_re)
        out_im.append(row_im)
    return out_re, out_im


def as_matrix(parts):
    return (
        [[parts[3 * i + j] for j in range(3)] for i in range(3)],
        [[parts[9 + 3 * i + j] for j in range(3)] for i in range(3)],
    )


def flat(matrix):
    return [matrix[0][i][j] for i in range(3) for j in range(3)] + [
        matrix[1][i][j] for i in range(3) for j in range(3)
    ]


def cmul(a, b):
    return a[0] * b[0] - a[1] * b[1], a[0] * b[1] + a[1] * b[0]


def zroll(value, step):
    return pltpu.roll(value, (-step) % value.shape[-1], value.ndim - 1)


def trace_kernel(own, own_s, tp, h, pm, out, v0, vup, trs):
    even = lax.broadcasted_iota(jnp.int32, (8, 128), 0) % 2 == 0

    def prep(i, _):
        for y in range(2):
            o = own[i, y]
            t = tp[i, y]
            v0[i, y, BASE : BASE + 8] = o
            v0[i, y, BASE + 8 : BASE + 10] = h[i, y, 2:4]
            vup[i, y] = jnp.where(even, pltpu.roll(o, 7, 0), pltpu.roll(t, 1, 0))
        v0[i, 2, BASE : BASE + 8] = own_s[i, 0]
        return 0

    lax.fori_loop(0, 72, prep, 0, unroll=4)
    trs[192:256] = jnp.zeros((64, 128), F32)

    def at_y(y, _):
        def look(d, step):
            if step == 0:
                parts = [vup[18 * d + c, y] for c in range(18)]
            elif step == 1:
                parts = [v0[18 * d + c, y, BASE + 2 : BASE + 10] for c in range(18)]
            elif step == 2:
                parts = [v0[18 * d + c, y + 1, BASE : BASE + 8] for c in range(18)]
            else:
                parts = [v0[18 * d + c, y, BASE : BASE + 8] for c in range(18)]
                if step == 3:
                    parts = [zroll(p, 1) for p in parts]
            return as_matrix(parts)

        for p, (m, n) in enumerate(PAIRS):
            a = flat(mm(look(m, None), look(n, m)))
            b = flat(mm(look(n, None), look(m, n)))
            re = im = None
            for k in range(9):
                r = a[k] * b[k] + a[9 + k] * b[9 + k]
                q = a[9 + k] * b[k] - a[k] * b[9 + k]
                re = r if re is None else re + r
                im = q if im is None else im + q
            keep = pm[p, y] * (1.0 / 3.0)
            row = pl.multiple_of(y * 8, 8)
            trs[pl.ds((2 * p) * 16 + row, 8)] = re * keep
            trs[pl.ds((2 * p + 1) * 16 + row, 8)] = im * keep
        return 0

    lax.fori_loop(0, 2, at_y, 0)
    for r in range(16):
        out[r] = trs[pl.ds(r, 16, stride=16), :].astype(BF16)


def staple_kernel(ya, own, own_s, tp, tp_s, h, h_s, co, co_s, out, v0, vup, vdn):
    even = lax.broadcasted_iota(jnp.int32, (8, 128), 0) % 2 == 0
    places = ((1, 1), (0, 0), (0, 1), (1, 0))

    def prep(i, _):
        for y, (other, at) in enumerate(places):
            o = (own, own_s)[other][i, at]
            t = (tp, tp_s)[other][i, at]
            hh = (h, h_s)[other]
            v0[i, y, BASE : BASE + 8] = o
            v0[i, y, BASE - 2 : BASE] = hh[i, at, 0:2]
            v0[i, y, BASE + 8 : BASE + 10] = hh[i, at, 2:4]
            vup[i, y, BASE : BASE + 8] = jnp.where(even, pltpu.roll(o, 7, 0), pltpu.roll(t, 1, 0))
            vdn[i, y, BASE : BASE + 8] = jnp.where(even, pltpu.roll(t, 7, 0), pltpu.roll(o, 1, 0))
        return 0

    lax.fori_loop(0, 72, prep, 0, unroll=4)

    def corner(c, _):
        for y, (other, at) in enumerate(places):
            hh, cc = (h, h_s)[other], (co, co_s)[other]
            vup[18 + c, y, BASE - 2 : BASE - 1] = hh[18 + c, at, 1:2]
            vup[18 + c, y, BASE - 1 : BASE] = cc[c, at, 0:1]
            vdn[c, y, BASE + 8 : BASE + 9] = cc[c, at, 1:2]
            vdn[c, y, BASE + 9 : BASE + 10] = hh[c, at, 2:3]
        return 0

    lax.fori_loop(0, 18, corner, 0, unroll=2)

    for m in range(4):
        yy = ya[m] + 1

        def look(d, offset):
            source = {0: v0, 1: vup, -1: vdn}[offset[0]]
            row = BASE + 2 * offset[1]
            parts = [source[18 * d + c, yy + offset[2], row : row + 8] for c in range(18)]
            if offset[3] != 0:
                parts = [zroll(p, offset[3]) for p in parts]
            return as_matrix(parts)

        zero = (0, 0, 0, 0)
        others = [n for n in range(4) if n != m]
        for j, n in enumerate(others):
            step_m = tuple(int(k == m) for k in range(4))
            step_n = tuple(int(k == n) for k in range(4))
            back_n = tuple(-k for k in step_n)
            corner_mn = tuple(a - b for a, b in zip(step_m, step_n))
            up = mm(look(n, step_m), mm(look(n, zero), look(m, step_n)), b_dag=True)
            for c, value in enumerate(flat(up)):
                out[6 * m + 2 * j, c] = value
            down = mm(mm(look(m, back_n), look(n, corner_mn)), look(n, back_n), a_dag=True)
            for c, value in enumerate(flat(down)):
                out[6 * m + 2 * j + 1, c] = value


def final_kernel(ya, own, staples, f, f_s, w_in, b_in, w_out, b_out, out, wts):
    places = ((1, 1), (0, 0), (0, 1), (1, 0))
    for y in range(2):
        for x in range(4):
            columns = []
            for t in range(2):
                tiles = []
                for a in range(3):
                    for b in range(3):
                        for c in range(3):
                            other, at = places[y + c]
                            tiles.append((f, f_s)[other][at, x + b, t + a])
                columns.append(jnp.concatenate(tiles, axis=0))
            patch = jnp.concatenate(columns, axis=1)
            g = jnp.dot(w_in[...], patch, preferred_element_type=F32)
            for t in range(2):
                lanes = slice(128 * t, 128 * t + 128)
                hidden = (
                    zroll(g[0:64, lanes], -1) + g[64:128, lanes] + zroll(g[128:192, lanes], 1)
                )
                hidden = jnp.tanh(hidden + b_in[...]).astype(BF16)
                weights = jnp.dot(w_out[...], hidden, preferred_element_type=F32) + b_out[...]
                row = 24 * (2 * x + t)
                wts[y, row : row + 24] = weights

    for m in range(4):
        y = ya[m]
        link = as_matrix([own[18 * m + c, y] for c in range(18)])
        total = None
        for k in range(6 * m, 6 * m + 6):
            w = wts[y, pl.ds(k, 8, stride=24), :]
            term = [w * staples[k, c] for c in range(18)]
            total = term if total is None else [a + b for a, b in zip(total, term)]
        are, aim = mm(link, as_matrix(total))
        trace_im = (aim[0][0] + aim[1][1] + aim[2][2]) * (1.0 / 3.0)
        low = [[None] * 3 for _ in range(3)]
        for i in range(3):
            low[i][i] = (jnp.ones_like(trace_im), -0.5 * (aim[i][i] - trace_im))
            for k in range(i + 1, 3):
                qr = -0.25 * (are[i][k] - are[k][i])
                qi = -0.25 * (aim[i][k] + aim[k][i])
                low[i][k] = (qr, qi)
                low[k][i] = (-qr, qi)
        adj_re, adj_im = [], []
        for i in range(3):
            row_re, row_im = [], []
            for j in range(3):
                first = cmul(low[(j + 1) % 3][(i + 1) % 3], low[(j + 2) % 3][(i + 2) % 3])
                second = cmul(low[(j + 1) % 3][(i + 2) % 3], low[(j + 2) % 3][(i + 1) % 3])
                row_re.append(first[0] - second[0])
                row_im.append(first[1] - second[1])
            adj_re.append(row_re)
            adj_im.append(row_im)
        det_re = det_im = None
        for k in range(3):
            product = cmul(low[0][k], (adj_re[k][0], adj_im[k][0]))
            det_re = product[0] if det_re is None else det_re + product[0]
            det_im = product[1] if det_im is None else det_im + product[1]
        twice = 2.0 / (det_re * det_re + det_im * det_im)
        scale_re = det_re * twice
        scale_im = -det_im * twice
        turned = flat(mm((adj_re, adj_im), link))
        current = flat(link)
        for c in range(9):
            re, im = cmul((turned[c], turned[9 + c]), (scale_re, scale_im))
            out[18 * m + c, y] = re - current[c]
            out[18 * m + 9 + c, y] = im - current[9 + c]
        for c in range(18):
            out[18 * m + c, 1 - y] = own[18 * m + c, 1 - y]


VM = pl.BlockSpec(memory_space=pltpu.VMEM)
SM = pl.BlockSpec(memory_space=pltpu.SMEM)
PARAMS = pltpu.CompilerParams(vmem_limit_bytes=LIMIT)


def run_traces(own, own_s, tp, h, pm):
    return pl.pallas_call(
        trace_kernel,
        out_shape=jax.ShapeDtypeStruct((16, 16, 128), BF16),
        in_specs=[VM] * 5,
        out_specs=VM,
        scratch_shapes=[
            pltpu.VMEM((72, 3, 24, 128), F32),
            pltpu.VMEM((72, 2, 8, 128), F32),
            pltpu.VMEM((256, 128), F32),
        ],
        compiler_params=PARAMS,
        cost_estimate=pl.CostEstimate(flops=8_000_000, bytes_accessed=2_000_000, transcendentals=0),
        name="traces",
    )(own, own_s, tp, h, pm)


def run_staples(ya, own, own_s, tp, tp_s, h, h_s, co, co_s):
    return pl.pallas_call(
        staple_kernel,
        out_shape=jax.ShapeDtypeStruct((24, 18, 8, 128), F32),
        in_specs=[SM] + [VM] * 8,
        out_specs=VM,
        scratch_shapes=[pltpu.VMEM((72, 4, 24, 128), F32)] * 3,
        compiler_params=PARAMS,
        cost_estimate=pl.CostEstimate(flops=20_000_000, bytes_accessed=5_000_000, transcendentals=0),
        name="staples",
    )(ya, own, own_s, tp, tp_s, h, h_s, co, co_s)


def run_final(ya, own, staples, f, f_s, w_in, b_in, w_out, b_out):
    return pl.pallas_call(
        final_kernel,
        out_shape=jax.ShapeDtypeStruct((72, 2, 8, 128), F32),
        in_specs=[SM] + [VM] * 8,
        out_specs=VM,
        scratch_shapes=[pltpu.VMEM((2, 192, 128), F32)],
        compiler_params=PARAMS,
        cost_estimate=pl.CostEstimate(flops=300_000_000, bytes_accessed=4_000_000, transcendentals=131072),
        name="rotate",
    )(ya, own, staples, f, f_s, w_in, b_in, w_out, b_out)


def step(value, axis, by):
    count = lax.axis_size(axis)
    return lax.ppermute(value, axis, [((i + by) % count, i) for i in range(count)])


def other_time(value, dim):
    if lax.axis_size("tm") == 2:
        return step(value, "tm", 1)
    up = step(lax.slice_in_dim(value, 0, 1, axis=dim), "tm", 1)
    down = step(lax.slice_in_dim(value, 1, 2, axis=dim), "tm", -1)
    return jnp.concatenate([up, down], axis=dim)


def exchange(own):
    tp = other_time(own.reshape(72, 2, 4, 2, 128), 3).reshape(own.shape)
    left = step(own[:, :, 6:8], "space", -1)
    right = step(own[:, :, 0:2], "space", 1)
    h = jnp.concatenate([left, right], axis=2)
    mixed = jnp.concatenate([left[18:36, :, 0:1], right[0:18, :, 1:2]], axis=2)
    co = other_time(mixed, 2)
    return tp, h, co


def traces_rim(tr):
    tp = other_time(tr, 2)
    full = jnp.concatenate([tp[:, :, 1:2], tr, tp[:, :, 0:1]], axis=2)
    left = step(full[:, 3:4], "space", -1)
    right = step(full[:, 0:1], "space", 1)
    return jnp.concatenate([left, full, right], axis=1)


def active_window(active_blocks):
    t_len, x_len, y_len = 2, 4, 2

    def blocks(axis, length, lo, hi):
        total = lax.axis_size(axis) * length
        at = (lax.axis_index(axis) * length + jnp.arange(lo, hi, dtype=jnp.int32)) % total
        return at // length, at

    t_block, _ = blocks("tm", t_len, -1, 3)
    x_block, _ = blocks("space", x_len, -1, 5)
    _, y_at = blocks("sub", y_len, -1, 3)
    y_block = 2 * y_at // y_len
    table = (active_blocks > 0).astype(F32)

    def pick(table, at, dim):
        hot = (at[:, None] == jnp.arange(table.shape[dim])[None]).astype(F32)
        return jnp.tensordot(table, hot, axes=((dim,), (1,)), precision=lax.Precision.HIGHEST)

    table = pick(table, x_block, 3)
    table = pick(table, t_block, 2)
    return pick(table, y_block, 2)


def plane_masks(active):
    frozen = 1.0 - active

    def at(m, d):
        start = [1, 1, 1]
        if d is not None and d < 3:
            start[(1, 0, 2)[d]] += 1
        a, b, c = start
        return frozen[:, m, a : a + 4, b : b + 2, c : c + 2]

    masks = jnp.stack([at(m, None) * at(n, m) * at(m, n) * at(n, None) for m, n in PAIRS], axis=1)
    masks = jnp.transpose(masks, (0, 1, 4, 2, 3)).reshape(2, 6, 2, 8, 1)
    return jnp.broadcast_to(masks, (2, 6, 2, 8, 128))


def per_device(gauge_links, active_blocks, conv_in, bias_in, conv_out, bias_out):
    own = jnp.transpose(gauge_links, (0, 1, 4, 3, 2, 5)).reshape(72, 2, 8, 128)
    active = active_window(active_blocks)
    pm = plane_masks(active)
    ya = (active[:, :, 1, 1, 1] < 0.5).astype(jnp.int32)
    w_in = jnp.transpose(conv_in.reshape(2, 3, 3, 3, 3, 12, 64), (0, 4, 6, 1, 2, 3, 5))
    w_in = jnp.pad(w_in, [(0, 0)] * 6 + [(0, 4)]).reshape(2, 192, 432)
    w_out = jnp.transpose(conv_out, (0, 2, 1))
    b_in = jnp.broadcast_to(bias_in[:, :, None], (2, 64, 128))
    b_out = jnp.broadcast_to(bias_out[:, :, None], (2, 24, 128))

    for layer in range(2):
        if layer == 1:
            incoming = step(own[:, :, 0:4], "space", 1)
            own = jnp.concatenate([own[:, :, 4:8], incoming], axis=2)
        own_s = step(own, "sub", 1)
        tp, h, co = exchange(own)
        h_s = step(h, "sub", 1)
        co_s = step(co, "sub", 1)
        tp_s = step(tp, "sub", 1)
        tr = run_traces(own, own_s, tp, h, pm[layer])
        f = traces_rim(tr.reshape(2, 4, 2, 16, 128))
        f_s = step(f, "sub", 1)
        staples = run_staples(ya[layer], own, own_s, tp, tp_s, h, h_s, co, co_s)
        own = run_final(
            ya[layer], own, staples, f, f_s, w_in[layer], b_in[layer], w_out[layer], b_out[layer]
        )
    out = own.reshape(4, 18, 2, 4, 2, 128)
    return jnp.transpose(out, (0, 1, 4, 3, 2, 5))


def solution(mesh):
    placed = (
        P(None, None, ("grp", "tm"), "space", "sub", None),
        P("grp", None, None, None, None),
        P(),
        P(),
        P(),
        P(),
    )
    return jax.shard_map(
        per_device,
        mesh=mesh,
        in_specs=placed,
        out_specs=P(None, None, ("grp", "tm"), "space", "sub", None),
        check_vma=False,
    )
```

```python
import jax
import jax.numpy as jnp
from jax import lax
from jax.experimental import pallas as pl
from jax.experimental.pallas import tpu as pltpu
from jax.sharding import PartitionSpec as P

PAIRS = ((0, 1), (0, 2), (0, 3), (1, 2), (1, 3), (2, 3))
F32 = jnp.float32
BF16 = jnp.bfloat16
BASE = 8


def mm(a, b, a_dag=False, b_dag=False):
    out_re, out_im = [], []
    for i in range(3):
        row_re, row_im = [], []
        for j in range(3):
            re = im = None
            for k in range(3):
                ar, ai = (a[0][k][i], a[1][k][i]) if a_dag else (a[0][i][k], a[1][i][k])
                br, bi = (b[0][j][k], b[1][j][k]) if b_dag else (b[0][k][j], b[1][k][j])
                if a_dag:
                    r, m = ar * br + ai * bi, ar * bi - ai * br
                elif b_dag:
                    r, m = ar * br + ai * bi, ai * br - ar * bi
                else:
                    r, m = ar * br - ai * bi, ar * bi + ai * br
                re = r if re is None else re + r
                im = m if im is None else im + m
            row_re.append(re)
            row_im.append(im)
        out_re.append(row_re)
        out_im.append(row_im)
    return out_re, out_im


def as_matrix(parts):
    return (
        [[parts[3 * i + j] for j in range(3)] for i in range(3)],
        [[parts[9 + 3 * i + j] for j in range(3)] for i in range(3)],
    )


def flat(matrix):
    return [matrix[0][i][j] for i in range(3) for j in range(3)] + [
        matrix[1][i][j] for i in range(3) for j in range(3)
    ]


def cmul(a, b):
    return a[0] * b[0] - a[1] * b[1], a[0] * b[1] + a[1] * b[0]


def zroll(value, step):
    return pltpu.roll(value, (-step) % value.shape[-1], value.ndim - 1)


def trace_kernel(ya, own, own_s, tp, h, out, v0, vup, trs):
    even = lax.broadcasted_iota(jnp.int32, (8, 128), 0) % 2 == 0

    def prep(i, _):
        for y in range(2):
            o = own[i, y]
            t = tp[i, y]
            v0[i, y, BASE : BASE + 8] = o
            v0[i, y, BASE + 8 : BASE + 10] = h[i, y, 2:4]
            vup[i, y] = jnp.where(even, pltpu.roll(o, 7, 0), pltpu.roll(t, 1, 0))
        v0[i, 2, BASE : BASE + 8] = own_s[i, 0]
        return 0

    lax.fori_loop(0, 72, prep, 0, unroll=4)
    trs[192:256] = jnp.zeros((64, 128), F32)
    row_of = lax.broadcasted_iota(jnp.int32, (8, 128), 0)
    leaves = (row_of % 2, jnp.where(row_of >= 6, 1, 0), 1, 0)

    def at_y(y, _):
        active = [jnp.where(ya[m] == y, 1, 0) for m in range(4)]

        def look(d, step):
            if step == 0:
                parts = [vup[18 * d + c, y] for c in range(18)]
            elif step == 1:
                parts = [v0[18 * d + c, y, BASE + 2 : BASE + 10] for c in range(18)]
            elif step == 2:
                parts = [v0[18 * d + c, y + 1, BASE : BASE + 8] for c in range(18)]
            else:
                parts = [v0[18 * d + c, y, BASE : BASE + 8] for c in range(18)]
                if step == 3:
                    parts = [zroll(p, 1) for p in parts]
            return as_matrix(parts)

        for p, (m, n) in enumerate(PAIRS):
            a = flat(mm(look(m, None), look(n, m)))
            b = flat(mm(look(n, None), look(m, n)))
            re = im = None
            for k in range(9):
                r = a[k] * b[k] + a[9 + k] * b[9 + k]
                q = a[9 + k] * b[k] - a[k] * b[9 + k]
                re = r if re is None else re + r
                im = q if im is None else im + q
            moved = (active[n] ^ leaves[m]) | (active[m] ^ leaves[n]) | active[m] | active[n]
            frozen = jnp.broadcast_to(moved, (8, 128)) == 0
            row = pl.multiple_of(y * 8, 8)
            trs[pl.ds((2 * p) * 16 + row, 8)] = jnp.where(frozen, re * (1.0 / 3.0), 0.0)
            trs[pl.ds((2 * p + 1) * 16 + row, 8)] = jnp.where(frozen, im * (1.0 / 3.0), 0.0)
        return 0

    lax.fori_loop(0, 2, at_y, 0)
    for r in range(16):
        out[r] = trs[pl.ds(r, 16, stride=16), :].astype(BF16)


def staple_kernel(ya, own, own_s, tp, tp_s, h, h_s, co, co_s, out, v0, vup, vdn):
    even = lax.broadcasted_iota(jnp.int32, (8, 128), 0) % 2 == 0
    places = ((1, 1), (0, 0), (0, 1), (1, 0))

    def prep(i, _):
        for y, (other, at) in enumerate(places):
            o = (own, own_s)[other][i, at]
            t = (tp, tp_s)[other][i, at]
            hh = (h, h_s)[other]
            v0[i, y, BASE : BASE + 8] = o
            v0[i, y, BASE - 2 : BASE] = hh[i, at, 0:2]
            v0[i, y, BASE + 8 : BASE + 10] = hh[i, at, 2:4]
            vup[i, y, BASE : BASE + 8] = jnp.where(even, pltpu.roll(o, 7, 0), pltpu.roll(t, 1, 0))
            vdn[i, y, BASE : BASE + 8] = jnp.where(even, pltpu.roll(t, 7, 0), pltpu.roll(o, 1, 0))
        return 0

    lax.fori_loop(0, 72, prep, 0, unroll=4)

    def corner(c, _):
        for y, (other, at) in enumerate(places):
            hh, cc = (h, h_s)[other], (co, co_s)[other]
            vup[18 + c, y, BASE - 2 : BASE - 1] = hh[18 + c, at, 1:2]
            vup[18 + c, y, BASE - 1 : BASE] = cc[c, at, 0:1]
            vdn[c, y, BASE + 8 : BASE + 9] = cc[c, at, 1:2]
            vdn[c, y, BASE + 9 : BASE + 10] = hh[c, at, 2:3]
        return 0

    lax.fori_loop(0, 18, corner, 0, unroll=2)

    for m in range(4):
        yy = ya[m] + 1

        def look(d, offset):
            source = {0: v0, 1: vup, -1: vdn}[offset[0]]
            row = BASE + 2 * offset[1]
            parts = [source[18 * d + c, yy + offset[2], row : row + 8] for c in range(18)]
            if offset[3] != 0:
                parts = [zroll(p, offset[3]) for p in parts]
            return as_matrix(parts)

        zero = (0, 0, 0, 0)
        others = [n for n in range(4) if n != m]
        for j, n in enumerate(others):
            step_m = tuple(int(k == m) for k in range(4))
            step_n = tuple(int(k == n) for k in range(4))
            back_n = tuple(-k for k in step_n)
            corner_mn = tuple(a - b for a, b in zip(step_m, step_n))
            up = mm(look(n, step_m), mm(look(n, zero), look(m, step_n)), b_dag=True)
            for c, value in enumerate(flat(up)):
                out[6 * m + 2 * j, c] = value
            down = mm(mm(look(m, back_n), look(n, corner_mn)), look(n, back_n), a_dag=True)
            for c, value in enumerate(flat(down)):
                out[6 * m + 2 * j + 1, c] = value


def unpack_kernel(x, own, first, last):
    def body(i, _):
        for y in range(2):
            for t in range(2):
                own[i, y, pl.ds(t, 4, stride=2)] = x[i, pl.ds(8 * t + y, 4, stride=2)]
                first[i, y, t : t + 1] = x[i, 8 * t + y : 8 * t + y + 1]
                last[i, y, t : t + 1] = x[i, 8 * t + 6 + y : 8 * t + 7 + y]
        return 0

    lax.fori_loop(0, 72, body, 0, unroll=8)


def weights_kernel(conv_in, bias_in, conv_out, bias_out, *refs):
    outs, big, small = refs[:8], refs[8], refs[9]
    big[...] = jnp.zeros_like(big)
    small[...] = jnp.zeros_like(small)
    for layer in range(2):
        w_in, b_in, w_out, b_out = outs[4 * layer : 4 * layer + 4]
        for k in range(27):
            taps = [conv_in[layer, 3 * k + z].astype(F32) for z in range(3)]
            big[16 * k : 16 * k + 12, 0:192] = jnp.concatenate(taps, axis=1)
        w_in[...] = jnp.transpose(big[...])[0:192, 0:432].astype(BF16)
        small[0:64, 0:24] = conv_out[layer].astype(F32)
        w_out[...] = jnp.transpose(small[...])[0:24, 0:64].astype(BF16)
        small[:, 0:64] = jnp.broadcast_to(bias_in[layer : layer + 1], (128, 64))
        b_in[...] = jnp.transpose(small[...])[0:64]
        small[:, 0:24] = jnp.broadcast_to(bias_out[layer : layer + 1], (128, 24))
        b_out[...] = jnp.transpose(small[...])[0:24]


def last_kernel(ya, own, staples, f, f_s, w_in, b_in, w_out, b_out, packed, out, wts):
    final_kernel(ya, own, staples, f, f_s, w_in, b_in, w_out, b_out, out, wts)

    def body(i, _):
        for y in range(2):
            for t in range(2):
                packed[i, pl.ds(8 * t + y, 4, stride=2)] = out[i, y, pl.ds(t, 4, stride=2)]
        return 0

    lax.fori_loop(0, 72, body, 0, unroll=8)


def final_kernel(ya, own, staples, f, f_s, w_in, b_in, w_out, b_out, out, wts):
    places = ((1, 1), (0, 0), (0, 1), (1, 0))
    for y in range(2):
        for x in range(4):
            columns = []
            for t in range(2):
                tiles = []
                for a in range(3):
                    for b in range(3):
                        for c in range(3):
                            other, at = places[y + c]
                            tiles.append((f, f_s)[other][at, x + b, t + a])
                columns.append(jnp.concatenate(tiles, axis=0))
            patch = jnp.concatenate(columns, axis=1)
            g = jnp.dot(w_in[...], patch, preferred_element_type=F32)
            for t in range(2):
                lanes = slice(128 * t, 128 * t + 128)
                hidden = (
                    zroll(g[0:64, lanes], -1) + g[64:128, lanes] + zroll(g[128:192, lanes], 1)
                )
                hidden = jnp.tanh(hidden + b_in[...]).astype(BF16)
                weights = jnp.dot(w_out[...], hidden, preferred_element_type=F32) + b_out[...]
                row = 24 * (2 * x + t)
                wts[y, row : row + 24] = weights

    for m in range(4):
        y = ya[m]
        link = as_matrix([own[18 * m + c, y] for c in range(18)])
        total = None
        for k in range(6 * m, 6 * m + 6):
            w = wts[y, pl.ds(k, 8, stride=24), :]
            term = [w * staples[k, c] for c in range(18)]
            total = term if total is None else [a + b for a, b in zip(total, term)]
        are, aim = mm(link, as_matrix(total))
        trace_im = (aim[0][0] + aim[1][1] + aim[2][2]) * (1.0 / 3.0)
        low = [[None] * 3 for _ in range(3)]
        for i in range(3):
            low[i][i] = (jnp.ones_like(trace_im), -0.5 * (aim[i][i] - trace_im))
            for k in range(i + 1, 3):
                qr = -0.25 * (are[i][k] - are[k][i])
                qi = -0.25 * (aim[i][k] + aim[k][i])
                low[i][k] = (qr, qi)
                low[k][i] = (-qr, qi)
        adj_re, adj_im = [], []
        for i in range(3):
            row_re, row_im = [], []
            for j in range(3):
                first = cmul(low[(j + 1) % 3][(i + 1) % 3], low[(j + 2) % 3][(i + 2) % 3])
                second = cmul(low[(j + 1) % 3][(i + 2) % 3], low[(j + 2) % 3][(i + 1) % 3])
                row_re.append(first[0] - second[0])
                row_im.append(first[1] - second[1])
            adj_re.append(row_re)
            adj_im.append(row_im)
        det_re = det_im = None
        for k in range(3):
            product = cmul(low[0][k], (adj_re[k][0], adj_im[k][0]))
            det_re = product[0] if det_re is None else det_re + product[0]
            det_im = product[1] if det_im is None else det_im + product[1]
        twice = 2.0 / (det_re * det_re + det_im * det_im)
        scale_re = det_re * twice
        scale_im = -det_im * twice
        turned = flat(mm((adj_re, adj_im), link))
        current = flat(link)
        for c in range(9):
            re, im = cmul((turned[c], turned[9 + c]), (scale_re, scale_im))
            out[18 * m + c, y] = re - current[c]
            out[18 * m + 9 + c, y] = im - current[9 + c]
        for c in range(18):
            out[18 * m + c, 1 - y] = own[18 * m + c, 1 - y]


VM = pl.BlockSpec(memory_space=pltpu.VMEM)
SM = pl.BlockSpec(memory_space=pltpu.SMEM)


def params(mib):
    return pltpu.CompilerParams(vmem_limit_bytes=mib * 1024 * 1024)


def run_weights(conv_in, bias_in, conv_out, bias_out):
    shapes = [((192, 432), BF16), ((64, 128), F32), ((24, 64), BF16), ((24, 128), F32)]
    return pl.pallas_call(
        weights_kernel,
        out_shape=[jax.ShapeDtypeStruct(*shape) for shape in shapes * 2],
        in_specs=[VM] * 4,
        out_specs=[VM] * 8,
        scratch_shapes=[pltpu.VMEM((512, 256), F32), pltpu.VMEM((128, 128), F32)],
        compiler_params=params(8),
        cost_estimate=pl.CostEstimate(flops=0, bytes_accessed=6_000_000, transcendentals=0),
        name="weights",
    )(conv_in, bias_in, conv_out, bias_out)


def run_unpack(x):
    rows = jax.ShapeDtypeStruct((72, 2, 2, 128), F32)
    return pl.pallas_call(
        unpack_kernel,
        out_shape=[jax.ShapeDtypeStruct((72, 2, 8, 128), F32), rows, rows],
        in_specs=[VM],
        out_specs=[VM] * 3,
        compiler_params=params(8),
        cost_estimate=pl.CostEstimate(flops=0, bytes_accessed=2_000_000, transcendentals=0),
        name="unpack",
    )(x)


def run_traces(ya, own, own_s, tp, h):
    return pl.pallas_call(
        trace_kernel,
        out_shape=jax.ShapeDtypeStruct((16, 16, 128), BF16),
        in_specs=[SM] + [VM] * 4,
        out_specs=VM,
        scratch_shapes=[
            pltpu.VMEM((72, 3, 24, 128), F32),
            pltpu.VMEM((72, 2, 8, 128), F32),
            pltpu.VMEM((256, 128), F32),
        ],
        compiler_params=params(16),
        cost_estimate=pl.CostEstimate(flops=8_000_000, bytes_accessed=2_000_000, transcendentals=0),
        name="traces",
    )(ya, own, own_s, tp, h)


def run_staples(ya, own, own_s, tp, tp_s, h, h_s, co, co_s):
    return pl.pallas_call(
        staple_kernel,
        out_shape=jax.ShapeDtypeStruct((24, 18, 8, 128), F32),
        in_specs=[SM] + [VM] * 8,
        out_specs=VM,
        scratch_shapes=[pltpu.VMEM((72, 4, 24, 128), F32)] * 3,
        compiler_params=params(22),
        cost_estimate=pl.CostEstimate(flops=20_000_000, bytes_accessed=16_000_000, transcendentals=0),
        name="staples",
    )(ya, own, own_s, tp, tp_s, h, h_s, co, co_s)


def run_final(ya, own, staples, f, f_s, w_in, b_in, w_out, b_out, last):
    weights = [pltpu.VMEM((2, 192, 128), F32)]
    return pl.pallas_call(
        last_kernel if last else final_kernel,
        out_shape=jax.ShapeDtypeStruct((72, 16, 128) if last else (72, 2, 8, 128), F32),
        in_specs=[SM] + [VM] * 8,
        out_specs=VM,
        scratch_shapes=([pltpu.VMEM((72, 2, 8, 128), F32)] if last else []) + weights,
        compiler_params=params(14),
        cost_estimate=pl.CostEstimate(flops=300_000_000, bytes_accessed=4_000_000, transcendentals=131072),
        name="rotate",
    )(ya, own, staples, f, f_s, w_in, b_in, w_out, b_out)


def step(value, axis, by):
    count = lax.axis_size(axis)
    return lax.ppermute(value, axis, [((i + by) % count, i) for i in range(count)])


def other_time(value, dim):
    if lax.axis_size("tm") == 2:
        return step(value, "tm", 1)
    up = step(lax.slice_in_dim(value, 0, 1, axis=dim), "tm", 1)
    down = step(lax.slice_in_dim(value, 1, 2, axis=dim), "tm", -1)
    return jnp.concatenate([up, down], axis=dim)


def diagonal(value, x_by, t_by):
    n_x, n_t = lax.axis_size("space"), lax.axis_size("tm")
    pairs = [
        ((i + x_by) % n_x * n_t + (k + t_by) % n_t, i * n_t + k)
        for i in range(n_x)
        for k in range(n_t)
    ]
    return lax.ppermute(value, ("space", "tm"), pairs)


def exchange(own, first, last):
    tp = other_time(own.reshape(72, 2, 4, 2, 128), 3).reshape(own.shape)
    left = step(last, "space", -1)
    right = step(first, "space", 1)
    co_left = diagonal(last[18:36, :, 0:1], -1, 1)
    co_right = diagonal(first[0:18, :, 1:2], 1, -1)
    return tp, left, right, co_left, co_right


def traces_rim(tr, meanwhile):
    tp = other_time(tr, 2)
    full = jnp.concatenate([tp[:, :, 1:2], tr, tp[:, :, 0:1]], axis=2)
    left = step(full[:, 3:4], "space", -1)
    right = step(full[:, 0:1], "space", 1)
    other = meanwhile()
    left, right, other = lax.optimization_barrier((left, right, other))
    return jnp.concatenate([left, full, right], axis=1), other


def active_rows(active_blocks):
    index = (lax.axis_index("tm"), lax.axis_index("space"), 2 * lax.axis_index("sub"))
    at = lax.dynamic_slice(active_blocks, (0, 0) + index, active_blocks.shape[:2] + (1, 1, 1))
    return jnp.where(at[:, :, 0, 0, 0] > 0, 0, 1).astype(jnp.int32)


def per_device(gauge_links, active_blocks, conv_in, bias_in, conv_out, bias_out):
    own, first, last = run_unpack(gauge_links.reshape(72, 16, 128))
    ya = active_rows(active_blocks)
    weights = run_weights(conv_in, bias_in, conv_out, bias_out)
    for layer in range(2):
        if layer == 1:
            incoming = step(own[:, :, 0:4], "space", 1)
            own = jnp.concatenate([own[:, :, 4:8], incoming], axis=2)
            first, last = own[:, :, 0:2], own[:, :, 6:8]
        own_s = step(own, "sub", 1)
        tp, left, right, co_left, co_right = exchange(own, first, last)
        if layer == 0:
            left, right, ya, weights = lax.optimization_barrier((left, right, ya, weights))
            ya = [ya[0], ya[1]]
        h = jnp.concatenate([left, right], axis=2)
        co = jnp.concatenate([co_left, co_right], axis=2)
        h_s = step(h, "sub", 1)
        co_s = step(co, "sub", 1)
        tp, h_s, co_s = lax.optimization_barrier((tp, h_s, co_s))
        tp_s = step(tp, "sub", 1)
        tr = run_traces(ya[layer], own, own_s, tp, h)
        links = (own, own_s, tp, tp_s, h, h_s, co, co_s)
        f, staples = traces_rim(
            tr.reshape(2, 4, 2, 16, 128), lambda: run_staples(ya[layer], *links)
        )
        f_s = step(f, "sub", 1)
        own = run_final(
            ya[layer],
            own,
            staples,
            f,
            f_s,
            *weights[4 * layer : 4 * layer + 4],
            layer == 1,
        )
    return own.reshape(4, 18, 2, 4, 2, 128)


def solution(mesh):
    placed = (
        P(None, None, ("grp", "tm"), "space", "sub", None),
        P("grp", None, None, None, None),
        P(),
        P(),
        P(),
        P(),
    )
    return jax.shard_map(
        per_device,
        mesh=mesh,
        in_specs=placed,
        out_specs=P(None, None, ("grp", "tm"), "space", "sub", None),
        check_vma=False,
    )
```

```python
import functools

import jax
import jax.numpy as jnp
from jax import lax
from jax.experimental import pallas as pl
from jax.experimental.pallas import tpu as pltpu
from jax.sharding import PartitionSpec as P

PAIRS = ((0, 1), (0, 2), (0, 3), (1, 2), (1, 3), (2, 3))
F32 = jnp.float32
BF16 = jnp.bfloat16
BASE = 8


def mm(a, b, a_dag=False, b_dag=False):
    out_re, out_im = [], []
    for i in range(3):
        row_re, row_im = [], []
        for j in range(3):
            re = im = None
            for k in range(3):
                ar, ai = (a[0][k][i], a[1][k][i]) if a_dag else (a[0][i][k], a[1][i][k])
                br, bi = (b[0][j][k], b[1][j][k]) if b_dag else (b[0][k][j], b[1][k][j])
                if a_dag:
                    r, m = ar * br + ai * bi, ar * bi - ai * br
                elif b_dag:
                    r, m = ar * br + ai * bi, ai * br - ar * bi
                else:
                    r, m = ar * br - ai * bi, ar * bi + ai * br
                re = r if re is None else re + r
                im = m if im is None else im + m
            row_re.append(re)
            row_im.append(im)
        out_re.append(row_re)
        out_im.append(row_im)
    return out_re, out_im


def as_matrix(parts):
    return (
        [[parts[3 * i + j] for j in range(3)] for i in range(3)],
        [[parts[9 + 3 * i + j] for j in range(3)] for i in range(3)],
    )


def flat(matrix):
    return [matrix[0][i][j] for i in range(3) for j in range(3)] + [
        matrix[1][i][j] for i in range(3) for j in range(3)
    ]


def cmul(a, b):
    return a[0] * b[0] - a[1] * b[1], a[0] * b[1] + a[1] * b[0]


def zroll(value, step):
    return pltpu.roll(value, (-step) % value.shape[-1], value.ndim - 1)


def trace_kernel(at_right, halves, ya, *refs):
    inputs, (out, v0, vup, trs) = refs[:-4], refs[-4:]
    if halves == 1:
        own, own_s, tp, right = inputs
        parts = [(own, own_s, tp, right, at_right)]
    else:
        own, own_s, tp, right, tp_s, right_tp = inputs
        parts = [(own, own_s, tp, right, at_right), (tp, tp_s, own, right_tp, 0)]
    even = lax.broadcasted_iota(jnp.int32, (8, 128), 0) % 2 == 0
    count = 16 * halves

    def prep(i, _):
        for half, (link, link_s, later, after, at) in enumerate(parts):
            k = 72 * half + i
            for y in range(2):
                o = link[i, y]
                t = later[i, y]
                v0[k, y, BASE : BASE + 8] = o
                v0[k, y, BASE + 8 : BASE + 10] = after[i, y, at : at + 2]
                vup[k, y] = jnp.where(even, pltpu.roll(o, 7, 0), pltpu.roll(t, 1, 0))
            v0[k, 2, BASE : BASE + 8] = link_s[i, 0]
        return 0

    lax.fori_loop(0, 72, prep, 0, unroll=4)
    trs[12 * count :] = jnp.zeros((4 * count, 128), F32)
    row_of = lax.broadcasted_iota(jnp.int32, (8, 128), 0)
    leaves = (row_of % 2, jnp.where(row_of >= 6, 1, 0), 1, 0)

    def at_y(place, _):
        half, y = place // 2, place % 2
        active = [jnp.where(ya[m] == y, 1, 0) ^ half for m in range(4)]
        first = 72 * half

        def look(d, step):
            base = first + 18 * d
            if step == 0:
                parts = [vup[base + c, y] for c in range(18)]
            elif step == 1:
                parts = [v0[base + c, y, BASE + 2 : BASE + 10] for c in range(18)]
            elif step == 2:
                parts = [v0[base + c, y + 1, BASE : BASE + 8] for c in range(18)]
            else:
                parts = [v0[base + c, y, BASE : BASE + 8] for c in range(18)]
                if step == 3:
                    parts = [zroll(p, 1) for p in parts]
            return as_matrix(parts)

        for p, (m, n) in enumerate(PAIRS):
            a = flat(mm(look(m, None), look(n, m)))
            b = flat(mm(look(n, None), look(m, n)))
            re = im = None
            for k in range(9):
                r = a[k] * b[k] + a[9 + k] * b[9 + k]
                q = a[9 + k] * b[k] - a[k] * b[9 + k]
                re = r if re is None else re + r
                im = q if im is None else im + q
            moved = (active[n] ^ leaves[m]) | (active[m] ^ leaves[n]) | active[m] | active[n]
            frozen = jnp.broadcast_to(moved, (8, 128)) == 0
            row = pl.multiple_of(place * 8, 8)
            trs[pl.ds((2 * p) * count + row, 8)] = jnp.where(frozen, re * (1.0 / 3.0), 0.0)
            trs[pl.ds((2 * p + 1) * count + row, 8)] = jnp.where(frozen, im * (1.0 / 3.0), 0.0)
        return 0

    lax.fori_loop(0, 2 * halves, at_y, 0)
    for r in range(count):
        half, yx, t = r // 16, r % 16 // 2, r % 2
        place = r if halves == 1 else 4 * yx + ((3, 0)[t] if half else 1 + t)
        out[place] = trs[pl.ds(r, 16, stride=count), :].astype(BF16)


def staple_kernel(ya, own, own_s, tp, tp_s, h, h_s, co, co_s, out, v0, vup, vdn):
    even = lax.broadcasted_iota(jnp.int32, (8, 128), 0) % 2 == 0
    places = ((1, 1), (0, 0), (0, 1), (1, 0))

    def prep(i, _):
        for y, (other, at) in enumerate(places):
            o = (own, own_s)[other][i, at]
            t = (tp, tp_s)[other][i, at]
            hh = (h, h_s)[other]
            v0[i, y, BASE : BASE + 8] = o
            v0[i, y, BASE - 2 : BASE] = hh[i, at, 0:2]
            v0[i, y, BASE + 8 : BASE + 10] = hh[i, at, 2:4]
            vup[i, y, BASE : BASE + 8] = jnp.where(even, pltpu.roll(o, 7, 0), pltpu.roll(t, 1, 0))
            vdn[i, y, BASE : BASE + 8] = jnp.where(even, pltpu.roll(t, 7, 0), pltpu.roll(o, 1, 0))
        return 0

    lax.fori_loop(0, 72, prep, 0, unroll=4)

    def corner(c, _):
        for y, (other, at) in enumerate(places):
            hh, cc = (h, h_s)[other], (co, co_s)[other]
            vup[18 + c, y, BASE - 2 : BASE - 1] = hh[18 + c, at, 1:2]
            vup[18 + c, y, BASE - 1 : BASE] = cc[c, at, 0:1]
            vdn[c, y, BASE + 8 : BASE + 9] = cc[c, at, 1:2]
            vdn[c, y, BASE + 9 : BASE + 10] = hh[c, at, 2:3]
        return 0

    lax.fori_loop(0, 18, corner, 0, unroll=2)

    for m in range(4):
        yy = ya[m] + 1

        def look(d, offset):
            source = {0: v0, 1: vup, -1: vdn}[offset[0]]
            row = BASE + 2 * offset[1]
            parts = [source[18 * d + c, yy + offset[2], row : row + 8] for c in range(18)]
            if offset[3] != 0:
                parts = [zroll(p, offset[3]) for p in parts]
            return as_matrix(parts)

        zero = (0, 0, 0, 0)
        others = [n for n in range(4) if n != m]
        for j, n in enumerate(others):
            step_m = tuple(int(k == m) for k in range(4))
            step_n = tuple(int(k == n) for k in range(4))
            back_n = tuple(-k for k in step_n)
            corner_mn = tuple(a - b for a, b in zip(step_m, step_n))
            up = mm(look(n, step_m), mm(look(n, zero), look(m, step_n)), b_dag=True)
            for c, value in enumerate(flat(up)):
                out[6 * m + 2 * j, c] = value
            down = mm(mm(look(m, back_n), look(n, corner_mn)), look(n, back_n), a_dag=True)
            for c, value in enumerate(flat(down)):
                out[6 * m + 2 * j + 1, c] = value


def unpack_kernel(x, own, last, head):
    def body(i, _):
        for y in range(2):
            for t in range(2):
                own[i, y, pl.ds(t, 4, stride=2)] = x[i, pl.ds(8 * t + y, 4, stride=2)]
                head[i, y, pl.ds(t, 3, stride=2)] = x[i, pl.ds(8 * t + y, 3, stride=2)]
                last[i, y, t : t + 1] = x[i, 8 * t + 6 + y : 8 * t + 7 + y]
        return 0

    lax.fori_loop(0, 72, body, 0, unroll=8)


def weights_kernel(conv_in, bias_in, conv_out, bias_out, *refs):
    outs, big, small = refs[:8], refs[8], refs[9]
    big[...] = jnp.zeros_like(big)
    small[...] = jnp.zeros_like(small)
    for layer in range(2):
        w_in, b_in, w_out, b_out = outs[4 * layer : 4 * layer + 4]
        for k in range(27):
            taps = [conv_in[layer, 3 * k + z].astype(F32) for z in range(3)]
            big[16 * k : 16 * k + 12, 0:192] = jnp.concatenate(taps, axis=1)
        w_in[...] = jnp.transpose(big[...])[0:192, 0:432].astype(BF16)
        small[0:64, 0:24] = conv_out[layer].astype(F32)
        w_out[...] = jnp.transpose(small[...])[0:24, 0:64].astype(BF16)
        small[:, 0:64] = jnp.broadcast_to(bias_in[layer : layer + 1], (128, 64))
        b_in[...] = jnp.transpose(small[...])[0:64]
        small[:, 0:24] = jnp.broadcast_to(bias_out[layer : layer + 1], (128, 24))
        b_out[...] = jnp.transpose(small[...])[0:24]


def last_kernel(ya, own, staples, f, f_s, w_in, b_in, w_out, b_out, packed, out, wts):
    update(ya, own, staples, f, f_s, w_in, b_in, w_out, b_out, out, wts)

    def body(i, _):
        for y in range(2):
            for t in range(2):
                packed[i, pl.ds(8 * t + y, 4, stride=2)] = out[i, y, pl.ds(t, 4, stride=2)]
        return 0

    lax.fori_loop(0, 72, body, 0, unroll=8)


def final_kernel(
    ya, own, staples, f, f_s, w_in, b_in, w_out, b_out, out, q_head, q_tail, wts
):
    update(
        ya, own, staples, f, f_s, w_in, b_in, w_out, b_out, out, wts, sent=(q_head, q_tail)
    )


def update(ya, own, staples, f, f_s, w_in, b_in, w_out, b_out, out, wts, sent=None):
    places = ((1, 1), (0, 0), (0, 1), (1, 0))
    for y in range(2):
        for x in range(4):
            columns = []
            for t in range(2):
                tiles = []
                for a in range(3):
                    for b in range(3):
                        for c in range(3):
                            other, at = places[y + c]
                            tiles.append((f, f_s)[other][at, x + b, t + a])
                columns.append(jnp.concatenate(tiles, axis=0))
            patch = jnp.concatenate(columns, axis=1)
            g = jnp.dot(w_in[...], patch, preferred_element_type=F32)
            for t in range(2):
                lanes = slice(128 * t, 128 * t + 128)
                hidden = (
                    zroll(g[0:64, lanes], -1) + g[64:128, lanes] + zroll(g[128:192, lanes], 1)
                )
                hidden = jnp.tanh(hidden + b_in[...]).astype(BF16)
                weights = jnp.dot(w_out[...], hidden, preferred_element_type=F32) + b_out[...]
                row = 24 * (2 * x + t)
                wts[y, row : row + 24] = weights

    for m in range(4):
        y = ya[m]
        link = as_matrix([own[18 * m + c, y] for c in range(18)])
        total = None
        for k in range(6 * m, 6 * m + 6):
            w = wts[y, pl.ds(k, 8, stride=24), :]
            term = [w * staples[k, c] for c in range(18)]
            total = term if total is None else [a + b for a, b in zip(total, term)]
        are, aim = mm(link, as_matrix(total))
        trace_im = (aim[0][0] + aim[1][1] + aim[2][2]) * (1.0 / 3.0)
        low = []
        for i, k in ((0, 1), (0, 2), (1, 2)):
            low.append(-0.25 * (are[i][k] - are[k][i]))
            low.append(-0.25 * (aim[i][k] + aim[k][i]))
        low += [-0.5 * (aim[i][i] - trace_im) for i in range(3)]
        if sent is not None:
            for c in range(9):
                sent[0][9 * m + c] = low[c][0:6]
                sent[1][9 * m + c] = low[c][2:8]
        for c, value in enumerate(rotated(low, link)):
            out[18 * m + c, y] = value
        for c in range(18):
            out[18 * m + c, 1 - y] = own[18 * m + c, 1 - y]


def rotated(low, link):
    one = jnp.ones_like(low[0])
    full = [[None] * 3 for _ in range(3)]
    for i in range(3):
        full[i][i] = (one, low[6 + i])
    for at, (i, k) in enumerate(((0, 1), (0, 2), (1, 2))):
        re, im = low[2 * at], low[2 * at + 1]
        full[i][k] = (re, im)
        full[k][i] = (-re, im)
    adj_re, adj_im = [], []
    for i in range(3):
        row_re, row_im = [], []
        for j in range(3):
            first = cmul(full[(j + 1) % 3][(i + 1) % 3], full[(j + 2) % 3][(i + 2) % 3])
            second = cmul(full[(j + 1) % 3][(i + 2) % 3], full[(j + 2) % 3][(i + 1) % 3])
            row_re.append(first[0] - second[0])
            row_im.append(first[1] - second[1])
        adj_re.append(row_re)
        adj_im.append(row_im)
    det_re = det_im = None
    for k in range(3):
        product = cmul(full[0][k], (adj_re[k][0], adj_im[k][0]))
        det_re = product[0] if det_re is None else det_re + product[0]
        det_im = product[1] if det_im is None else det_im + product[1]
    twice = 2.0 / (det_re * det_re + det_im * det_im)
    scale_re = det_re * twice
    scale_im = -det_im * twice
    turned = flat(mm((adj_re, adj_im), link))
    current = flat(link)
    real, imag = [], []
    for c in range(9):
        re, im = cmul((turned[c], turned[9 + c]), (scale_re, scale_im))
        real.append(re - current[c])
        imag.append(im - current[9 + c])
    return real + imag


def shift_kernel(ya, own, head, tp, far, q_head, q_tp, q_far, own_o, h_o, tp_o, co_o, right_tp_o):
    for m in range(4):
        here = ya[m]
        there = 1 - here
        rows = slice(18 * m, 18 * m + 18)

        def turn(q, links):
            return rotated([q[9 * m + c] for c in range(9)], as_matrix(links))

        new = turn(q_head, [head[i, there] for i in range(rows.start, rows.stop)])
        for c, i in enumerate(range(rows.start, rows.stop)):
            for y in range(2):
                own_o[i, y, 0:4] = own[i, y, 4:8]
                h_o[i, y, 0:2] = own[i, y, 2:4]
            own_o[i, there, 4:8] = new[c][0:4]
            h_o[i, there, 2:4] = new[c][4:6]
            own_o[i, here, 4:8] = head[i, here, 0:4]
            h_o[i, here, 2:4] = head[i, here, 4:6]
        new = turn(q_tp, [tp[i, there, 2:8] for i in range(rows.start, rows.stop)])
        for c, i in enumerate(range(rows.start, rows.stop)):
            tp_o[i, there, 0:4] = new[c][2:6]
            tp_o[i, here, 0:4] = tp[i, here, 4:8]
            if m == 1:
                co_o[c, there, 0:1] = new[c][0:1]
                co_o[c, here, 0:1] = tp[i, here, 2:3]
        new = turn(q_far, [far[i, here] for i in range(rows.start, rows.stop)])
        for c, i in enumerate(range(rows.start, rows.stop)):
            tp_o[i, here, 4:8] = new[c][0:4]
            tp_o[i, there, 4:8] = far[i, there, 0:4]
            right_tp_o[i, here] = new[c][4:6]
            right_tp_o[i, there] = far[i, there, 4:6]
            if m == 0:
                co_o[c, here, 1:2] = new[c][5:6]
                co_o[c, there, 1:2] = far[i, there, 5:6]


VM = pl.BlockSpec(memory_space=pltpu.VMEM)
SM = pl.BlockSpec(memory_space=pltpu.SMEM)


def params(mib):
    return pltpu.CompilerParams(vmem_limit_bytes=mib * 1024 * 1024)


def run_weights(conv_in, bias_in, conv_out, bias_out):
    shapes = [((192, 432), BF16), ((64, 128), F32), ((24, 64), BF16), ((24, 128), F32)]
    return pl.pallas_call(
        weights_kernel,
        out_shape=[jax.ShapeDtypeStruct(*shape) for shape in shapes * 2],
        in_specs=[VM] * 4,
        out_specs=[VM] * 8,
        scratch_shapes=[pltpu.VMEM((512, 256), F32), pltpu.VMEM((128, 128), F32)],
        compiler_params=params(8),
        cost_estimate=pl.CostEstimate(flops=0, bytes_accessed=6_000_000, transcendentals=0),
        name="weights",
    )(conv_in, bias_in, conv_out, bias_out)


def run_unpack(x):
    return pl.pallas_call(
        unpack_kernel,
        out_shape=[
            jax.ShapeDtypeStruct((72, 2, 8, 128), F32),
            jax.ShapeDtypeStruct((72, 2, 2, 128), F32),
            jax.ShapeDtypeStruct((72, 2, 6, 128), F32),
        ],
        in_specs=[VM],
        out_specs=[VM] * 3,
        compiler_params=params(8),
        cost_estimate=pl.CostEstimate(flops=0, bytes_accessed=2_000_000, transcendentals=0),
        name="unpack",
    )(x)


def run_traces(ya, at_right, *inputs):
    halves = 1 if len(inputs) == 4 else 2
    return pl.pallas_call(
        functools.partial(trace_kernel, at_right, halves),
        out_shape=jax.ShapeDtypeStruct((16 * halves, 16, 128), BF16),
        in_specs=[SM] + [VM] * len(inputs),
        out_specs=VM,
        scratch_shapes=[
            pltpu.VMEM((72 * halves, 3, 24, 128), F32),
            pltpu.VMEM((72 * halves, 2, 8, 128), F32),
            pltpu.VMEM((256 * halves, 128), F32),
        ],
        compiler_params=params(8 + 8 * halves),
        cost_estimate=pl.CostEstimate(flops=8_000_000, bytes_accessed=6_000_000, transcendentals=0),
        name="traces",
    )(ya, *inputs)


def run_staples(ya, own, own_s, tp, tp_s, h, h_s, co, co_s):
    return pl.pallas_call(
        staple_kernel,
        out_shape=jax.ShapeDtypeStruct((24, 18, 8, 128), F32),
        in_specs=[SM] + [VM] * 8,
        out_specs=VM,
        scratch_shapes=[pltpu.VMEM((72, 4, 24, 128), F32)] * 3,
        compiler_params=params(22),
        cost_estimate=pl.CostEstimate(flops=20_000_000, bytes_accessed=16_000_000, transcendentals=0),
        name="staples",
    )(ya, own, own_s, tp, tp_s, h, h_s, co, co_s)


def run_final(ya, own, staples, f, f_s, w_in, b_in, w_out, b_out, last):
    weights = [pltpu.VMEM((2, 192, 128), F32)]
    shapes = [(72, 16, 128)] if last else [(72, 2, 8, 128), (36, 6, 128), (36, 6, 128)]
    return pl.pallas_call(
        last_kernel if last else final_kernel,
        out_shape=[jax.ShapeDtypeStruct(shape, F32) for shape in shapes],
        in_specs=[SM] + [VM] * 8,
        out_specs=[VM] * len(shapes),
        scratch_shapes=([pltpu.VMEM((72, 2, 8, 128), F32)] if last else []) + weights,
        compiler_params=params(14),
        cost_estimate=pl.CostEstimate(flops=300_000_000, bytes_accessed=4_000_000, transcendentals=131072),
        name="rotate",
    )(ya, own, staples, f, f_s, w_in, b_in, w_out, b_out)


def run_shift(ya, *arrays):
    shapes = [(72, 2, 8, 128), (72, 2, 4, 128), (72, 2, 8, 128), (18, 2, 2, 128), (72, 2, 2, 128)]
    return pl.pallas_call(
        shift_kernel,
        out_shape=[jax.ShapeDtypeStruct(shape, F32) for shape in shapes],
        in_specs=[SM] + [VM] * 7,
        out_specs=[VM] * 5,
        compiler_params=params(10),
        cost_estimate=pl.CostEstimate(flops=8_000_000, bytes_accessed=6_000_000, transcendentals=0),
        name="shift",
    )(ya, *arrays)


def step(value, axis, by):
    count = lax.axis_size(axis)
    return lax.ppermute(value, axis, [((i + by) % count, i) for i in range(count)])


def diagonal(value, x_by, t_by):
    n_x, n_t = lax.axis_size("space"), lax.axis_size("tm")
    pairs = [
        ((i + x_by) % n_x * n_t + (k + t_by) % n_t, i * n_t + k)
        for i in range(n_x)
        for k in range(n_t)
    ]
    return lax.ppermute(value, ("space", "tm"), pairs)


def other_time(value, dim, x_by=0):
    if lax.axis_size("tm") == 2:
        return diagonal(value, x_by, 1)
    up = diagonal(lax.slice_in_dim(value, 0, 1, axis=dim), x_by, 1)
    down = diagonal(lax.slice_in_dim(value, 1, 2, axis=dim), x_by, -1)
    return jnp.concatenate([up, down], axis=dim)


def other_rows(value, x_by=0):
    split = value.reshape(value.shape[:-2] + (value.shape[-2] // 2, 2, 128))
    return other_time(split, split.ndim - 2, x_by).reshape(value.shape)


def active_rows(active_blocks):
    index = (lax.axis_index("tm"), lax.axis_index("space"), 2 * lax.axis_index("sub"))
    at = lax.dynamic_slice(active_blocks, (0, 0) + index, active_blocks.shape[:2] + (1, 1, 1))
    return jnp.where(at[:, :, 0, 0, 0] > 0, 0, 1).astype(jnp.int32)


def per_device(gauge_links, active_blocks, conv_in, bias_in, conv_out, bias_out):
    own, last, head = run_unpack(gauge_links.reshape(72, 16, 128))
    ya = active_rows(active_blocks)
    weights = run_weights(conv_in, bias_in, conv_out, bias_out)

    tp = other_rows(own)
    head = step(head, "space", 1)
    left = step(last, "space", -1)
    own_s = step(own, "sub", 1)
    head, left, ya, weights = lax.optimization_barrier((head, left, ya, weights))
    ya = [ya[0], ya[1]]
    mixed = jnp.concatenate([left[18:36, :, 0:1], head[0:18, :, 1:2]], axis=2)
    h = jnp.concatenate([left, head[:, :, 0:2]], axis=2)
    co = other_time(mixed, 2)
    tr = run_traces(ya[0], 0, own, own_s, tp, head).reshape(2, 4, 2, 16, 128)
    full = other_traces(tr)
    full, co, h = lax.optimization_barrier((full, co, h))
    own, q_head, q_tail = rest(full, own, own_s, tp, h, co, ya[0], weights[:4], False)
    far = other_rows(head)

    own, h, tp, co, right_tp = run_shift(
        ya[0],
        own,
        head,
        tp,
        far,
        step(q_head, "space", 1),
        other_rows(q_tail),
        other_rows(q_head, 1),
    )

    own_s, tp_s = step(own, "sub", 1), step(tp, "sub", 1)
    if lax.axis_size("tm") == 2:
        full = run_traces(ya[1], 2, own, own_s, tp, h, tp_s, right_tp)
        full = full.reshape(2, 4, 4, 16, 128)
    else:
        full = other_traces(run_traces(ya[1], 2, own, own_s, tp, h).reshape(2, 4, 2, 16, 128))
    (own,) = rest(full, own, own_s, tp, h, co, ya[1], weights[4:], True, tp_s)
    return own.reshape(4, 18, 2, 4, 2, 128)


def other_traces(tr):
    times = other_time(tr, 2)
    return jnp.concatenate([times[:, :, 1:2], tr, times[:, :, 0:1]], axis=2)


def rest(full, own, own_s, tp, h, co, ya, weights, last, tp_s=None):
    before = step(full[:, 3:4], "space", -1)
    after = step(full[:, 0:1], "space", 1)
    if tp_s is None:
        tp_s = step(tp, "sub", 1)
    h_s, co_s = step(h, "sub", 1), step(co, "sub", 1)
    staples = run_staples(ya, own, own_s, tp, tp_s, h, h_s, co, co_s)
    before, after, staples = lax.optimization_barrier((before, after, staples))
    f = jnp.concatenate([before, full, after], axis=1)
    f_s = step(f, "sub", 1)
    return run_final(ya, own, staples, f, f_s, *weights, last)


def solution(mesh):
    placed = (
        P(None, None, ("grp", "tm"), "space", "sub", None),
        P("grp", None, None, None, None),
        P(),
        P(),
        P(),
        P(),
    )
    return jax.shard_map(
        per_device,
        mesh=mesh,
        in_specs=placed,
        out_specs=P(None, None, ("grp", "tm"), "space", "sub", None),
        check_vma=False,
    )
```

```python
import functools

import jax
import jax.numpy as jnp
from jax import lax
from jax.experimental import pallas as pl
from jax.experimental.pallas import tpu as pltpu
from jax.sharding import PartitionSpec as P

PAIRS = ((0, 1), (0, 2), (0, 3), (1, 2), (1, 3), (2, 3))
F32 = jnp.float32
BF16 = jnp.bfloat16
BASE = 8


def mm(a, b, a_dag=False, b_dag=False):
    out_re, out_im = [], []
    for i in range(3):
        row_re, row_im = [], []
        for j in range(3):
            re = im = None
            for k in range(3):
                ar, ai = (a[0][k][i], a[1][k][i]) if a_dag else (a[0][i][k], a[1][i][k])
                br, bi = (b[0][j][k], b[1][j][k]) if b_dag else (b[0][k][j], b[1][k][j])
                if a_dag:
                    r, m = ar * br + ai * bi, ar * bi - ai * br
                elif b_dag:
                    r, m = ar * br + ai * bi, ai * br - ar * bi
                else:
                    r, m = ar * br - ai * bi, ar * bi + ai * br
                re = r if re is None else re + r
                im = m if im is None else im + m
            row_re.append(re)
            row_im.append(im)
        out_re.append(row_re)
        out_im.append(row_im)
    return out_re, out_im


def as_matrix(parts):
    return (
        [[parts[3 * i + j] for j in range(3)] for i in range(3)],
        [[parts[9 + 3 * i + j] for j in range(3)] for i in range(3)],
    )


def flat(matrix):
    return [matrix[0][i][j] for i in range(3) for j in range(3)] + [
        matrix[1][i][j] for i in range(3) for j in range(3)
    ]


def cmul(a, b):
    return a[0] * b[0] - a[1] * b[1], a[0] * b[1] + a[1] * b[0]


def zroll(value, step):
    return pltpu.roll(value, (-step) % value.shape[-1], value.ndim - 1)


def trace_kernel(mode, ya, *refs):
    if mode == "single":
        own, own_s, tp, right, out, trs, placed = refs

        def place(i, _):
            for y in range(2):
                placed[i, y, 6:8] = right[i, y]
            return 0

        lax.fori_loop(0, 72, place, 0, unroll=8)
    else:
        packs, ex, out, trs = refs[:3], refs[3], refs[4], refs[5]
    wide = mode == "wide"
    parts = 3 if wide else 1
    count = 16 * parts
    row_of = lax.broadcasted_iota(jnp.int32, (8, 128), 0)
    even = row_of % 2 == 0

    def links(part, y, i):
        if mode == "single":
            return own_s[i, 0] if y == 2 else (own, tp)[part][i, y]
        return packs[y][72 * part + i]

    def later(part, y, i):
        o = links(part, y, i)
        t = pltpu.roll(o, 4, 0) if part == 2 else links(1 - part, y, i)
        return jnp.where(even, pltpu.roll(o, 7, 0), pltpu.roll(t, 1, 0))

    def right_of(part, y, i):
        if part == 2:
            return ex[i, y]
        if mode == "single":
            after = placed[i, y]
        else:
            after = links(2, y, i)
            after = pltpu.roll(after, 4, 0) if part == 0 else after
        return jnp.where(row_of < 6, pltpu.roll(links(part, y, i), 6, 0), after)

    trs[12 * count :] = jnp.zeros((4 * count, 128), F32)
    for part in range(parts):
        inner = jnp.where(row_of >= 6, 1, 0)
        leaves = (row_of % 2, 1 - row_of // 2 % 2 if part == 2 else inner, 1, 0)
        flip = jnp.where(row_of < 4, 1, 0) if part == 2 else part
        for y in range(2):
            active = [jnp.where(ya[m] == y, 1, 0) ^ flip for m in range(4)]

            def look(d, step):
                at = range(18 * d, 18 * d + 18)
                if step == 0:
                    return as_matrix([later(part, y, i) for i in at])
                if step == 1:
                    return as_matrix([right_of(part, y, i) for i in at])
                if step == 2:
                    return as_matrix([links(part, y + 1, i) for i in at])
                values = [links(part, y, i) for i in at]
                return as_matrix([zroll(v, 1) for v in values] if step == 3 else values)

            for p, (m, n) in enumerate(PAIRS):
                a = flat(mm(look(m, None), look(n, m)))
                b = flat(mm(look(n, None), look(m, n)))
                re = im = None
                for k in range(9):
                    r = a[k] * b[k] + a[9 + k] * b[9 + k]
                    q = a[9 + k] * b[k] - a[k] * b[9 + k]
                    re = r if re is None else re + r
                    im = q if im is None else im + q
                moved = (active[n] ^ leaves[m]) | (active[m] ^ leaves[n]) | active[m] | active[n]
                frozen = jnp.broadcast_to(moved, (8, 128)) == 0
                for k, value in enumerate((re, im)):
                    row = (2 * p + k) * count + 16 * part + 8 * y
                    trs[row : row + 8] = jnp.where(frozen, value * (1.0 / 3.0), 0.0)
    for r in range(count):
        place = r
        if wide:
            part, y, row = r // 16, r // 8 % 2, r % 8
            if part < 2:
                partner, x = part, 1 + row // 2
            else:
                partner, x = row // 4, (0, 5)[row // 2 % 2]
            t = (3, 0)[row % 2] if partner else 1 + row % 2
            place = (6 * y + x) * 4 + t
        out[place] = trs[pl.ds(r, 16, stride=count), :].astype(BF16)


def staple_kernel(mode, ya, *refs):
    inputs, (out, v0, vup, vdn) = refs[:-4], refs[-4:]
    even = lax.broadcasted_iota(jnp.int32, (8, 128), 0) % 2 == 0
    places = ((1, 1), (0, 0), (0, 1), (1, 0))
    if mode == "single":
        own, own_s, tp, tp_s, h, h_s, co, co_s = inputs

    def prep(i, _):
        for y, (other, at) in enumerate(places):
            if mode == "single":
                o, t = (own, own_s)[other][i, at], (tp, tp_s)[other][i, at]
                hh = (h, h_s)[other][i, at]
            else:
                pack = inputs[2 * other + at]
                o, t, hh = pack[i], pack[72 + i], pack[144 + i]
            v0[i, y, BASE : BASE + 8] = o
            v0[i, y, BASE - 2 : BASE] = hh[0:2]
            v0[i, y, BASE + 8 : BASE + 10] = hh[2:4]
            vup[i, y, BASE : BASE + 8] = jnp.where(even, pltpu.roll(o, 7, 0), pltpu.roll(t, 1, 0))
            vdn[i, y, BASE : BASE + 8] = jnp.where(even, pltpu.roll(t, 7, 0), pltpu.roll(o, 1, 0))
        return 0

    lax.fori_loop(0, 72, prep, 0, unroll=4)

    def corner(c, _):
        for y, (other, at) in enumerate(places):
            if mode == "single":
                hh, cc = (h, h_s)[other], (co, co_s)[other]
                x_links = hh[18 + c, at, 1:2], cc[c, at, 0:1]
                t_links = cc[c, at, 1:2], hh[c, at, 2:3]
            else:
                pack = inputs[2 * other + at]
                x_links = pack[162 + c, 1:2], pack[162 + c, 4:5]
                t_links = pack[144 + c, 7:8], pack[144 + c, 2:3]
            vup[18 + c, y, BASE - 2 : BASE - 1] = x_links[0]
            vup[18 + c, y, BASE - 1 : BASE] = x_links[1]
            vdn[c, y, BASE + 8 : BASE + 9] = t_links[0]
            vdn[c, y, BASE + 9 : BASE + 10] = t_links[1]
        return 0

    lax.fori_loop(0, 18, corner, 0, unroll=2)

    for m in range(4):
        yy = ya[m] + 1

        def look(d, offset):
            source = {0: v0, 1: vup, -1: vdn}[offset[0]]
            row = BASE + 2 * offset[1]
            parts = [source[18 * d + c, yy + offset[2], row : row + 8] for c in range(18)]
            if offset[3] != 0:
                parts = [zroll(p, offset[3]) for p in parts]
            return as_matrix(parts)

        zero = (0, 0, 0, 0)
        others = [n for n in range(4) if n != m]
        for j, n in enumerate(others):
            step_m = tuple(int(k == m) for k in range(4))
            step_n = tuple(int(k == n) for k in range(4))
            back_n = tuple(-k for k in step_n)
            corner_mn = tuple(a - b for a, b in zip(step_m, step_n))
            up = mm(look(n, step_m), mm(look(n, zero), look(m, step_n)), b_dag=True)
            for c, value in enumerate(flat(up)):
                out[6 * m + 2 * j, c] = value
            down = mm(mm(look(m, back_n), look(n, corner_mn)), look(n, back_n), a_dag=True)
            for c, value in enumerate(flat(down)):
                out[6 * m + 2 * j + 1, c] = value


def unpack_kernel(x, own, *rows):
    def body(i, _):
        for y in range(2):
            for t in range(2):
                at = 8 * t + y
                own[i, y, pl.ds(t, 4, stride=2)] = x[i, pl.ds(at, 4, stride=2)]
                if rows:
                    rows[0][i, y, t : t + 1] = x[i, at : at + 1]
                    rows[1][i, y, t : t + 1] = x[i, at + 6 : at + 7]
        return 0

    lax.fori_loop(0, 72, body, 0, unroll=8)


def tail_kernel(own, tail):
    def body(i, _):
        for y in range(2):
            tail[i, y] = own[i, y, 2:8]
        return 0

    lax.fori_loop(0, 72, body, 0, unroll=8)


def weights_kernel(conv_in, bias_in, conv_out, bias_out, *refs):
    outs, big, small = refs[:8], refs[8], refs[9]
    big[...] = jnp.zeros_like(big)
    small[...] = jnp.zeros_like(small)
    for layer in range(2):
        w_in, b_in, w_out, b_out = outs[4 * layer : 4 * layer + 4]
        for k in range(27):
            taps = [conv_in[layer, 3 * k + z].astype(F32) for z in range(3)]
            big[16 * k : 16 * k + 12, 0:192] = jnp.concatenate(taps, axis=1)
        w_in[...] = jnp.transpose(big[...])[0:192, 0:432].astype(BF16)
        small[0:64, 0:24] = conv_out[layer].astype(F32)
        w_out[...] = jnp.transpose(small[...])[0:24, 0:64].astype(BF16)
        small[:, 0:64] = jnp.broadcast_to(bias_in[layer : layer + 1], (128, 64))
        b_in[...] = jnp.transpose(small[...])[0:64]
        small[:, 0:24] = jnp.broadcast_to(bias_out[layer : layer + 1], (128, 24))
        b_out[...] = jnp.transpose(small[...])[0:24]


def last_kernel(ya, own, staples, f, f_s, w_in, b_in, w_out, b_out, packed, out, wts):
    update(ya, own, staples, f, f_s, w_in, b_in, w_out, b_out, out, wts)

    def body(i, _):
        for y in range(2):
            for t in range(2):
                packed[i, pl.ds(8 * t + y, 4, stride=2)] = out[i, y, pl.ds(t, 4, stride=2)]
        return 0

    lax.fori_loop(0, 72, body, 0, unroll=8)


def final_kernel(ya, own, staples, f, f_s, w_in, b_in, w_out, b_out, out, sent, wts):
    update(ya, own, staples, f, f_s, w_in, b_in, w_out, b_out, out, wts, sent)


def update(ya, own, staples, f, f_s, w_in, b_in, w_out, b_out, out, wts, sent=None):
    places = ((1, 1), (0, 0), (0, 1), (1, 0))
    for y in range(2):
        for x in range(4):
            columns = []
            for t in range(2):
                tiles = []
                for a in range(3):
                    for b in range(3):
                        for c in range(3):
                            other, at = places[y + c]
                            tiles.append((f, f_s)[other][at, x + b, t + a])
                columns.append(jnp.concatenate(tiles, axis=0))
            patch = jnp.concatenate(columns, axis=1)
            g = jnp.dot(w_in[...], patch, preferred_element_type=F32)
            for t in range(2):
                lanes = slice(128 * t, 128 * t + 128)
                hidden = (
                    zroll(g[0:64, lanes], -1) + g[64:128, lanes] + zroll(g[128:192, lanes], 1)
                )
                hidden = jnp.tanh(hidden + b_in[...]).astype(BF16)
                weights = jnp.dot(w_out[...], hidden, preferred_element_type=F32) + b_out[...]
                row = 24 * (2 * x + t)
                wts[y, row : row + 24] = weights

    for m in range(4):
        y = ya[m]
        link = as_matrix([own[18 * m + c, y] for c in range(18)])
        total = None
        for k in range(6 * m, 6 * m + 6):
            w = wts[y, pl.ds(k, 8, stride=24), :]
            term = [w * staples[k, c] for c in range(18)]
            total = term if total is None else [a + b for a, b in zip(total, term)]
        are, aim = mm(link, as_matrix(total))
        trace_im = (aim[0][0] + aim[1][1] + aim[2][2]) * (1.0 / 3.0)
        low = []
        for i, k in ((0, 1), (0, 2), (1, 2)):
            low.append(-0.25 * (are[i][k] - are[k][i]))
            low.append(-0.25 * (aim[i][k] + aim[k][i]))
        low += [-0.5 * (aim[i][i] - trace_im) for i in range(3)]
        if sent is not None:
            for c in range(9):
                sent[9 * m + c] = low[c]
        for c, value in enumerate(rotated(low, link)):
            out[18 * m + c, y] = value
        for c in range(18):
            out[18 * m + c, 1 - y] = own[18 * m + c, 1 - y]


def rotated(low, link):
    one = jnp.ones_like(low[0])
    full = [[None] * 3 for _ in range(3)]
    for i in range(3):
        full[i][i] = (one, low[6 + i])
    for at, (i, k) in enumerate(((0, 1), (0, 2), (1, 2))):
        re, im = low[2 * at], low[2 * at + 1]
        full[i][k] = (re, im)
        full[k][i] = (-re, im)
    adj_re, adj_im = [], []
    for i in range(3):
        row_re, row_im = [], []
        for j in range(3):
            first = cmul(full[(j + 1) % 3][(i + 1) % 3], full[(j + 2) % 3][(i + 2) % 3])
            second = cmul(full[(j + 1) % 3][(i + 2) % 3], full[(j + 2) % 3][(i + 1) % 3])
            row_re.append(first[0] - second[0])
            row_im.append(first[1] - second[1])
        adj_re.append(row_re)
        adj_im.append(row_im)
    det_re = det_im = None
    for k in range(3):
        product = cmul(full[0][k], (adj_re[k][0], adj_im[k][0]))
        det_re = product[0] if det_re is None else det_re + product[0]
        det_im = product[1] if det_im is None else det_im + product[1]
    twice = 2.0 / (det_re * det_re + det_im * det_im)
    scale_re = det_re * twice
    scale_im = -det_im * twice
    turned = flat(mm((adj_re, adj_im), link))
    current = flat(link)
    real, imag = [], []
    for c in range(9):
        re, im = cmul((turned[c], turned[9 + c]), (scale_re, scale_im))
        real.append(re - current[c])
        imag.append(im - current[9 + c])
    return real + imag


def shift_kernel(
    ya, own, right, tail, tp, far, far_tail, q_next, q_tp, q_far, own_o, pack_0, pack_1, ex
):
    for m in range(4):
        here = ya[m]
        there = 1 - here
        at = [18 * m + c for c in range(18)]

        def turn(q, links):
            return rotated([q[9 * m + c] for c in range(9)], as_matrix(links))

        def joined(one, more, y):
            return [jnp.concatenate([one[i, y], more[i, y]], axis=0) for i in at]

        at_0 = here == 0

        def by_y(i, if_here, if_there):
            return (
                (pack_0, jnp.where(at_0, if_here, if_there)),
                (pack_1, jnp.where(at_0, if_there, if_here)),
            )

        new, old = turn(q_next, joined(right, tail, there)), joined(right, tail, here)
        for c, i in enumerate(at):
            for y, (pack, rows) in enumerate(by_y(i, old[c], new[c])):
                block = jnp.concatenate([own[i, y, 4:8], rows[0:4]], axis=0)
                own_o[i, y] = block
                pack[i] = block
                pack[144 + i, 0:2] = own[i, y, 2:4]
                pack[144 + i, 2:4] = rows[4:6]
                ex[i, y, 0:2] = own[i, y, 4:6]
                ex[i, y, 2:4] = rows[6:8]
        new, old = turn(q_tp, [tp[i, there] for i in at]), [tp[i, here] for i in at]
        for c, i in enumerate(at):
            for y, (pack, rows) in enumerate(by_y(i, old[c], new[c])):
                pack[72 + i, 0:4] = rows[4:8]
                pack[144 + i, 4:6] = rows[2:4]
                ex[i, y, 4:6] = rows[4:6]
        new, old = turn(q_far, joined(far, far_tail, here)), joined(far, far_tail, there)
        for c, i in enumerate(at):
            for y, (pack, rows) in enumerate(by_y(i, new[c], old[c])):
                pack[72 + i, 4:8] = rows[0:4]
                pack[144 + i, 6:8] = rows[4:6]
                ex[i, y, 6:8] = rows[6:8]


VM = pl.BlockSpec(memory_space=pltpu.VMEM)
SM = pl.BlockSpec(memory_space=pltpu.SMEM)


def params(mib):
    return pltpu.CompilerParams(vmem_limit_bytes=mib * 1024 * 1024)


def run_weights(conv_in, bias_in, conv_out, bias_out):
    shapes = [((192, 432), BF16), ((64, 128), F32), ((24, 64), BF16), ((24, 128), F32)]
    return pl.pallas_call(
        weights_kernel,
        out_shape=[jax.ShapeDtypeStruct(*shape) for shape in shapes * 2],
        in_specs=[VM] * 4,
        out_specs=[VM] * 8,
        scratch_shapes=[pltpu.VMEM((512, 256), F32), pltpu.VMEM((128, 128), F32)],
        compiler_params=params(8),
        cost_estimate=pl.CostEstimate(flops=0, bytes_accessed=6_000_000, transcendentals=0),
        name="weights",
    )(conv_in, bias_in, conv_out, bias_out)


def run_unpack(x, rows):
    lengths = (8, 2, 2) if rows else (8,)
    return pl.pallas_call(
        unpack_kernel,
        out_shape=[jax.ShapeDtypeStruct((72, 2, n, 128), F32) for n in lengths],
        in_specs=[VM],
        out_specs=[VM] * len(lengths),
        compiler_params=params(8),
        cost_estimate=pl.CostEstimate(flops=0, bytes_accessed=2_000_000, transcendentals=0),
        name="unpack",
    )(x.reshape(72, 16, 128))


def run_tail(own):
    return pl.pallas_call(
        tail_kernel,
        out_shape=jax.ShapeDtypeStruct((72, 2, 6, 128), F32),
        in_specs=[VM],
        out_specs=VM,
        compiler_params=params(8),
        cost_estimate=pl.CostEstimate(flops=0, bytes_accessed=1_000_000, transcendentals=0),
        name="tail",
    )(own)


def run_traces(mode, ya, *inputs):
    parts = 3 if mode == "wide" else 1
    placed = [pltpu.VMEM((72, 2, 8, 128), F32)] if mode == "single" else []
    return pl.pallas_call(
        functools.partial(trace_kernel, mode),
        out_shape=jax.ShapeDtypeStruct((16 * parts, 16, 128), BF16),
        in_specs=[SM] + [VM] * len(inputs),
        out_specs=VM,
        scratch_shapes=[pltpu.VMEM((256 * parts, 128), F32)] + placed,
        compiler_params=params(10),
        cost_estimate=pl.CostEstimate(flops=8_000_000, bytes_accessed=6_000_000, transcendentals=0),
        name="traces",
    )(ya, *inputs)


def run_staples(mode, ya, *inputs):
    return pl.pallas_call(
        functools.partial(staple_kernel, mode),
        out_shape=jax.ShapeDtypeStruct((24, 18, 8, 128), F32),
        in_specs=[SM] + [VM] * len(inputs),
        out_specs=VM,
        scratch_shapes=[pltpu.VMEM((72, 4, 24, 128), F32)] * 3,
        compiler_params=params(22),
        cost_estimate=pl.CostEstimate(
            flops=20_000_000, bytes_accessed=16_000_000, transcendentals=0
        ),
        name="staples",
    )(ya, *inputs)


def run_final(ya, own, staples, f, f_s, w_in, b_in, w_out, b_out, last):
    weights = [pltpu.VMEM((2, 192, 128), F32)]
    shapes = [(72, 16, 128)] if last else [(72, 2, 8, 128), (36, 8, 128)]
    return pl.pallas_call(
        last_kernel if last else final_kernel,
        out_shape=[jax.ShapeDtypeStruct(shape, F32) for shape in shapes],
        in_specs=[SM] + [VM] * 8,
        out_specs=[VM] * len(shapes),
        scratch_shapes=([pltpu.VMEM((72, 2, 8, 128), F32)] if last else []) + weights,
        compiler_params=params(14),
        cost_estimate=pl.CostEstimate(flops=300_000_000, bytes_accessed=4_000_000, transcendentals=131072),
        name="rotate",
    )(ya, own, staples, f, f_s, w_in, b_in, w_out, b_out)


def run_shift(ya, *arrays):
    block, pack = (72, 2, 8, 128), (216, 8, 128)
    return pl.pallas_call(
        shift_kernel,
        out_shape=[jax.ShapeDtypeStruct(shape, F32) for shape in (block, pack, pack, block)],
        in_specs=[SM] + [VM] * 9,
        out_specs=[VM] * 4,
        compiler_params=params(12),
        cost_estimate=pl.CostEstimate(flops=8_000_000, bytes_accessed=6_000_000, transcendentals=0),
        name="shift",
    )(ya, *arrays)


def step(value, axis, by):
    count = lax.axis_size(axis)
    return lax.ppermute(value, axis, [((i + by) % count, i) for i in range(count)])


def diagonal(value, x_by, t_by):
    n_x, n_t = lax.axis_size("space"), lax.axis_size("tm")
    pairs = [
        ((i + x_by) % n_x * n_t + (k + t_by) % n_t, i * n_t + k)
        for i in range(n_x)
        for k in range(n_t)
    ]
    return lax.ppermute(value, ("space", "tm"), pairs)


def other_time(value, dim, x_by=0):
    if lax.axis_size("tm") == 2:
        return diagonal(value, x_by, 1)
    up = diagonal(lax.slice_in_dim(value, 0, 1, axis=dim), x_by, 1)
    down = diagonal(lax.slice_in_dim(value, 1, 2, axis=dim), x_by, -1)
    return jnp.concatenate([up, down], axis=dim)


def other_rows(value, x_by=0):
    split = value.reshape(value.shape[:-2] + (value.shape[-2] // 2, 2, 128))
    return other_time(split, split.ndim - 2, x_by).reshape(value.shape)


def active_rows(active_blocks):
    index = (lax.axis_index("tm"), lax.axis_index("space"), 2 * lax.axis_index("sub"))
    at = lax.dynamic_slice(active_blocks, (0, 0) + index, active_blocks.shape[:2] + (1, 1, 1))
    return jnp.where(at[:, :, 0, 0, 0] > 0, 0, 1).astype(jnp.int32)


def per_device(gauge_links, active_blocks, conv_in, bias_in, conv_out, bias_out):
    tp_raw = other_time(gauge_links, 2)
    own, first, last = run_unpack(gauge_links, True)
    ya = active_rows(active_blocks)
    weights = run_weights(conv_in, bias_in, conv_out, bias_out)

    right = step(first, "space", 1)
    left = step(last, "space", -1)
    tail = step(run_tail(own), "space", 1)
    own_s = step(own, "sub", 1)
    right, left, ya, weights = lax.optimization_barrier((right, left, ya, weights))
    ya = [ya[0], ya[1]]
    mixed = jnp.concatenate([left[18:36, :, 0:1], right[0:18, :, 1:2]], axis=2)
    co = other_time(mixed, 2)
    h = jnp.concatenate([left, right], axis=2)
    h_s = step(h, "sub", 1)
    (tp,) = run_unpack(tp_raw, False)
    tr = run_traces("single", ya[0], own, own_s, tp, right).reshape(2, 4, 2, 16, 128)
    far = other_rows(right)
    full = other_traces(tr)
    full, co, far, tail = lax.optimization_barrier((full, co, far, tail))
    far_tail = other_rows(tail)
    tp_s, co_s = step(tp, "sub", 1), step(co, "sub", 1)
    f, staples = rim(
        full, lambda: run_staples("single", ya[0], own, own_s, tp, tp_s, h, h_s, co, co_s)
    )
    f_s = step(f, "sub", 1)
    own, q = run_final(ya[0], own, staples, f, f_s, *weights[:4], False)

    own, pack_0, pack_1, ex = run_shift(
        ya[0],
        own,
        right,
        tail,
        tp,
        far,
        far_tail,
        step(q, "space", 1),
        other_rows(q),
        other_rows(q, 1),
    )

    other_0, other_1 = step(pack_0, "sub", 1), step(pack_1, "sub", 1)

    def staples_1():
        return run_staples("packs", ya[1], pack_0, pack_1, other_0, other_1)

    if lax.axis_size("tm") == 2:
        f = run_traces("wide", ya[1], pack_0, pack_1, other_0, ex).reshape(2, 6, 4, 16, 128)
        staples = staples_1()
    else:
        tr = run_traces("packs", ya[1], pack_0, pack_1, other_0, ex).reshape(2, 4, 2, 16, 128)
        f, staples = rim(other_traces(tr), staples_1)
    f_s = step(f, "sub", 1)
    (out,) = run_final(ya[1], own, staples, f, f_s, *weights[4:], True)
    return out.reshape(4, 18, 2, 4, 2, 128)


def other_traces(tr):
    times = other_time(tr, 2)
    return jnp.concatenate([times[:, :, 1:2], tr, times[:, :, 0:1]], axis=2)


def rim(full, meanwhile):
    before = step(full[:, 3:4], "space", -1)
    after = step(full[:, 0:1], "space", 1)
    other = meanwhile()
    before, after, other = lax.optimization_barrier((before, after, other))
    return jnp.concatenate([before, full, after], axis=1), other


def solution(mesh):
    placed = (
        P(None, None, ("grp", "tm"), "space", "sub", None),
        P("grp", None, None, None, None),
        P(),
        P(),
        P(),
        P(),
    )
    return jax.shard_map(
        per_device,
        mesh=mesh,
        in_specs=placed,
        out_specs=P(None, None, ("grp", "tm"), "space", "sub", None),
        check_vma=False,
    )
```

```python
import functools

import jax
import jax.numpy as jnp
from jax import lax
from jax.experimental import pallas as pl
from jax.experimental.pallas import tpu as pltpu
from jax.sharding import PartitionSpec as P

PAIRS = ((0, 1), (0, 2), (0, 3), (1, 2), (1, 3), (2, 3))
F32 = jnp.float32
BF16 = jnp.bfloat16
BASE = 8


def mm(a, b, a_dag=False, b_dag=False):
    out_re, out_im = [], []
    for i in range(3):
        row_re, row_im = [], []
        for j in range(3):
            re = im = None
            for k in range(3):
                ar, ai = (a[0][k][i], a[1][k][i]) if a_dag else (a[0][i][k], a[1][i][k])
                br, bi = (b[0][j][k], b[1][j][k]) if b_dag else (b[0][k][j], b[1][k][j])
                if a_dag:
                    r, m = ar * br + ai * bi, ar * bi - ai * br
                elif b_dag:
                    r, m = ar * br + ai * bi, ai * br - ar * bi
                else:
                    r, m = ar * br - ai * bi, ar * bi + ai * br
                re = r if re is None else re + r
                im = m if im is None else im + m
            row_re.append(re)
            row_im.append(im)
        out_re.append(row_re)
        out_im.append(row_im)
    return out_re, out_im


def as_matrix(parts):
    return (
        [[parts[3 * i + j] for j in range(3)] for i in range(3)],
        [[parts[9 + 3 * i + j] for j in range(3)] for i in range(3)],
    )


def flat(matrix):
    return [matrix[0][i][j] for i in range(3) for j in range(3)] + [
        matrix[1][i][j] for i in range(3) for j in range(3)
    ]


def cmul(a, b):
    return a[0] * b[0] - a[1] * b[1], a[0] * b[1] + a[1] * b[0]


def zroll(value, step):
    return pltpu.roll(value, (-step) % value.shape[-1], value.ndim - 1)


def trace_kernel(mode, ya, *refs):
    if mode == "single":
        own, own_s, tp, right, out, trs, placed = refs

        def place(i, _):
            for y in range(2):
                placed[i, y, 6:8] = right[i, y]
            return 0

        lax.fori_loop(0, 72, place, 0, unroll=8)
    else:
        packs, ex, out, trs = refs[:3], refs[3], refs[4], refs[5]
    wide = mode == "wide"
    parts = 3 if wide else 1
    count = 16 * parts
    row_of = lax.broadcasted_iota(jnp.int32, (8, 128), 0)
    even = row_of % 2 == 0

    def links(part, y, i):
        if mode == "single":
            return own_s[i, 0] if y == 2 else (own, tp)[part][i, y]
        return packs[y][72 * part + i]

    def later(part, y, i):
        o = links(part, y, i)
        t = pltpu.roll(o, 4, 0) if part == 2 else links(1 - part, y, i)
        return jnp.where(even, pltpu.roll(o, 7, 0), pltpu.roll(t, 1, 0))

    def right_of(part, y, i):
        if part == 2:
            return ex[i, y]
        if mode == "single":
            after = placed[i, y]
        else:
            after = links(2, y, i)
            after = pltpu.roll(after, 4, 0) if part == 0 else after
        return jnp.where(row_of < 6, pltpu.roll(links(part, y, i), 6, 0), after)

    trs[12 * count :] = jnp.zeros((4 * count, 128), F32)
    for part in range(parts):
        inner = jnp.where(row_of >= 6, 1, 0)
        leaves = (row_of % 2, 1 - row_of // 2 % 2 if part == 2 else inner, 1, 0)
        flip = jnp.where(row_of < 4, 1, 0) if part == 2 else part
        for y in range(2):
            active = [jnp.where(ya[m] == y, 1, 0) ^ flip for m in range(4)]

            def look(d, step):
                at = range(18 * d, 18 * d + 18)
                if step == 0:
                    return as_matrix([later(part, y, i) for i in at])
                if step == 1:
                    return as_matrix([right_of(part, y, i) for i in at])
                if step == 2:
                    return as_matrix([links(part, y + 1, i) for i in at])
                values = [links(part, y, i) for i in at]
                return as_matrix([zroll(v, 1) for v in values] if step == 3 else values)

            for p, (m, n) in enumerate(PAIRS):
                a = flat(mm(look(m, None), look(n, m)))
                b = flat(mm(look(n, None), look(m, n)))
                re = im = None
                for k in range(9):
                    r = a[k] * b[k] + a[9 + k] * b[9 + k]
                    q = a[9 + k] * b[k] - a[k] * b[9 + k]
                    re = r if re is None else re + r
                    im = q if im is None else im + q
                moved = (active[n] ^ leaves[m]) | (active[m] ^ leaves[n]) | active[m] | active[n]
                frozen = jnp.broadcast_to(moved, (8, 128)) == 0
                for k, value in enumerate((re, im)):
                    row = (2 * p + k) * count + 16 * part + 8 * y
                    trs[row : row + 8] = jnp.where(frozen, value * (1.0 / 3.0), 0.0)
    for r in range(count):
        place = r
        if wide:
            part, y, row = r // 16, r // 8 % 2, r % 8
            if part < 2:
                partner, x = part, 1 + row // 2
            else:
                partner, x = row // 4, (0, 5)[row // 2 % 2]
            t = (3, 0)[row % 2] if partner else 1 + row % 2
            place = (6 * y + x) * 4 + t
        out[place] = trs[pl.ds(r, 16, stride=count), :].astype(BF16)


def staple_kernel(mode, ya, *refs):
    inputs, (out, v0, vup, vdn) = refs[:-4], refs[-4:]
    even = lax.broadcasted_iota(jnp.int32, (8, 128), 0) % 2 == 0
    places = ((1, 1), (0, 0), (0, 1), (1, 0))
    if mode == "single":
        own, own_s, tp, tp_s, h, h_s, co, co_s = inputs

    def prep(i, _):
        for y, (other, at) in enumerate(places):
            if mode == "single":
                o, t = (own, own_s)[other][i, at], (tp, tp_s)[other][i, at]
                hh = (h, h_s)[other][i, at]
            else:
                pack = inputs[2 * other + at]
                o, t, hh = pack[i], pack[72 + i], pack[144 + i]
            v0[i, y, BASE : BASE + 8] = o
            v0[i, y, BASE - 2 : BASE] = hh[0:2]
            v0[i, y, BASE + 8 : BASE + 10] = hh[2:4]
            vup[i, y, BASE : BASE + 8] = jnp.where(even, pltpu.roll(o, 7, 0), pltpu.roll(t, 1, 0))
            vdn[i, y, BASE : BASE + 8] = jnp.where(even, pltpu.roll(t, 7, 0), pltpu.roll(o, 1, 0))
        return 0

    lax.fori_loop(0, 72, prep, 0, unroll=4)

    def corner(c, _):
        for y, (other, at) in enumerate(places):
            if mode == "single":
                hh, cc = (h, h_s)[other], (co, co_s)[other]
                x_links = hh[18 + c, at, 1:2], cc[c, at, 0:1]
                t_links = cc[c, at, 1:2], hh[c, at, 2:3]
            else:
                pack = inputs[2 * other + at]
                x_links = pack[162 + c, 1:2], pack[162 + c, 4:5]
                t_links = pack[144 + c, 7:8], pack[144 + c, 2:3]
            vup[18 + c, y, BASE - 2 : BASE - 1] = x_links[0]
            vup[18 + c, y, BASE - 1 : BASE] = x_links[1]
            vdn[c, y, BASE + 8 : BASE + 9] = t_links[0]
            vdn[c, y, BASE + 9 : BASE + 10] = t_links[1]
        return 0

    lax.fori_loop(0, 18, corner, 0, unroll=2)

    for m in range(4):
        yy = ya[m] + 1

        def look(d, offset):
            source = {0: v0, 1: vup, -1: vdn}[offset[0]]
            row = BASE + 2 * offset[1]
            parts = [source[18 * d + c, yy + offset[2], row : row + 8] for c in range(18)]
            if offset[3] != 0:
                parts = [zroll(p, offset[3]) for p in parts]
            return as_matrix(parts)

        zero = (0, 0, 0, 0)
        others = [n for n in range(4) if n != m]
        for j, n in enumerate(others):
            step_m = tuple(int(k == m) for k in range(4))
            step_n = tuple(int(k == n) for k in range(4))
            back_n = tuple(-k for k in step_n)
            corner_mn = tuple(a - b for a, b in zip(step_m, step_n))
            up = mm(look(n, step_m), mm(look(n, zero), look(m, step_n)), b_dag=True)
            for c, value in enumerate(flat(up)):
                out[6 * m + 2 * j, c] = value
            down = mm(mm(look(m, back_n), look(n, corner_mn)), look(n, back_n), a_dag=True)
            for c, value in enumerate(flat(down)):
                out[6 * m + 2 * j + 1, c] = value


def unpack_kernel(x, own, *rows):
    def body(i, _):
        for y in range(2):
            for t in range(2):
                at = 8 * t + y
                own[i, y, pl.ds(t, 4, stride=2)] = x[i, pl.ds(at, 4, stride=2)]
                if rows:
                    rows[0][i, y, t : t + 1] = x[i, at : at + 1]
                    rows[1][i, y, t : t + 1] = x[i, at + 6 : at + 7]
        return 0

    lax.fori_loop(0, 72, body, 0, unroll=8)


def tail_kernel(own, tail):
    def body(i, _):
        for y in range(2):
            tail[i, y] = own[i, y, 2:8]
        return 0

    lax.fori_loop(0, 72, body, 0, unroll=8)


def weights_kernel(conv_in, bias_in, conv_out, bias_out, *refs):
    outs, big, small = refs[:8], refs[8], refs[9]
    big[...] = jnp.zeros_like(big)
    small[...] = jnp.zeros_like(small)
    for layer in range(2):
        w_in, b_in, w_out, b_out = outs[4 * layer : 4 * layer + 4]
        for k in range(27):
            taps = [conv_in[layer, 3 * k + z].astype(F32) for z in range(3)]
            big[16 * k : 16 * k + 12, 0:192] = jnp.concatenate(taps, axis=1)
        w_in[...] = jnp.transpose(big[...])[0:192, 0:432].astype(BF16)
        small[0:64, 0:24] = conv_out[layer].astype(F32)
        w_out[...] = jnp.transpose(small[...])[0:24, 0:64].astype(BF16)
        small[:, 0:64] = jnp.broadcast_to(bias_in[layer : layer + 1], (128, 64))
        b_in[...] = jnp.transpose(small[...])[0:64]
        small[:, 0:24] = jnp.broadcast_to(bias_out[layer : layer + 1], (128, 24))
        b_out[...] = jnp.transpose(small[...])[0:24]


def last_kernel(ya, own, staples, f, f_s, w_in, b_in, w_out, b_out, packed, out, wts):
    update(ya, own, staples, f, f_s, w_in, b_in, w_out, b_out, out, wts)

    def body(i, _):
        for y in range(2):
            for t in range(2):
                packed[i, pl.ds(8 * t + y, 4, stride=2)] = out[i, y, pl.ds(t, 4, stride=2)]
        return 0

    lax.fori_loop(0, 72, body, 0, unroll=8)


def final_kernel(ya, own, staples, f, f_s, w_in, b_in, w_out, b_out, out, sent, wts):
    update(ya, own, staples, f, f_s, w_in, b_in, w_out, b_out, out, wts, sent)


def update(ya, own, staples, f, f_s, w_in, b_in, w_out, b_out, out, wts, sent=None):
    places = ((1, 1), (0, 0), (0, 1), (1, 0))
    sites = [(y, r // 2, r % 2) for y in range(2) for r in range(8)]
    columns = []
    for y, x, t in sites:
        tiles = []
        for a in range(3):
            for b in range(3):
                for c in range(3):
                    other, at = places[y + c]
                    tiles.append((f, f_s)[other][at, x + b, t + a])
        columns.append(jnp.concatenate(tiles, axis=0))
    g = jnp.dot(w_in[...], jnp.concatenate(columns, axis=1), preferred_element_type=F32)
    hidden = []
    for k in range(16):
        lanes = slice(128 * k, 128 * k + 128)
        part = zroll(g[0:64, lanes], -1) + g[64:128, lanes] + zroll(g[128:192, lanes], 1)
        hidden.append(jnp.tanh(part + b_in[...]).astype(BF16))
    weights = jnp.dot(w_out[...], jnp.concatenate(hidden, axis=1), preferred_element_type=F32)
    for k in range(16):
        row = 24 * (k % 8)
        wts[k // 8, row : row + 24] = weights[:, 128 * k : 128 * k + 128] + b_out[...]

    for m in range(4):
        y = ya[m]
        link = as_matrix([own[18 * m + c, y] for c in range(18)])
        total = None
        for k in range(6 * m, 6 * m + 6):
            w = wts[y, pl.ds(k, 8, stride=24), :]
            term = [w * staples[k, c] for c in range(18)]
            total = term if total is None else [a + b for a, b in zip(total, term)]
        are, aim = mm(link, as_matrix(total))
        trace_im = (aim[0][0] + aim[1][1] + aim[2][2]) * (1.0 / 3.0)
        low = []
        for i, k in ((0, 1), (0, 2), (1, 2)):
            low.append(-0.25 * (are[i][k] - are[k][i]))
            low.append(-0.25 * (aim[i][k] + aim[k][i]))
        low += [-0.5 * (aim[i][i] - trace_im) for i in range(3)]
        if sent is not None:
            for c in range(9):
                sent[9 * m + c] = low[c]
        for c, value in enumerate(rotated(low, link)):
            out[18 * m + c, y] = value
        for c in range(18):
            out[18 * m + c, 1 - y] = own[18 * m + c, 1 - y]


def rotated(low, link):
    one = jnp.ones_like(low[0])
    full = [[None] * 3 for _ in range(3)]
    for i in range(3):
        full[i][i] = (one, low[6 + i])
    for at, (i, k) in enumerate(((0, 1), (0, 2), (1, 2))):
        re, im = low[2 * at], low[2 * at + 1]
        full[i][k] = (re, im)
        full[k][i] = (-re, im)
    adj_re, adj_im = [], []
    for i in range(3):
        row_re, row_im = [], []
        for j in range(3):
            first = cmul(full[(j + 1) % 3][(i + 1) % 3], full[(j + 2) % 3][(i + 2) % 3])
            second = cmul(full[(j + 1) % 3][(i + 2) % 3], full[(j + 2) % 3][(i + 1) % 3])
            row_re.append(first[0] - second[0])
            row_im.append(first[1] - second[1])
        adj_re.append(row_re)
        adj_im.append(row_im)
    det_re = det_im = None
    for k in range(3):
        product = cmul(full[0][k], (adj_re[k][0], adj_im[k][0]))
        det_re = product[0] if det_re is None else det_re + product[0]
        det_im = product[1] if det_im is None else det_im + product[1]
    twice = 2.0 / (det_re * det_re + det_im * det_im)
    scale_re = det_re * twice
    scale_im = -det_im * twice
    turned = flat(mm((adj_re, adj_im), link))
    current = flat(link)
    real, imag = [], []
    for c in range(9):
        re, im = cmul((turned[c], turned[9 + c]), (scale_re, scale_im))
        real.append(re - current[c])
        imag.append(im - current[9 + c])
    return real + imag


def shift_kernel(
    ya, own, right, tail, tp, far, far_tail, q_next, q_tp, q_far, own_o, pack_0, pack_1, ex
):
    for m in range(4):
        here = ya[m]
        there = 1 - here
        at = [18 * m + c for c in range(18)]

        def turn(q, links):
            return rotated([q[9 * m + c] for c in range(9)], as_matrix(links))

        def joined(one, more, y):
            return [jnp.concatenate([one[i, y], more[i, y]], axis=0) for i in at]

        at_0 = here == 0

        def by_y(i, if_here, if_there):
            return (
                (pack_0, jnp.where(at_0, if_here, if_there)),
                (pack_1, jnp.where(at_0, if_there, if_here)),
            )

        new, old = turn(q_next, joined(right, tail, there)), joined(right, tail, here)
        for c, i in enumerate(at):
            for y, (pack, rows) in enumerate(by_y(i, old[c], new[c])):
                block = jnp.concatenate([own[i, y, 4:8], rows[0:4]], axis=0)
                own_o[i, y] = block
                pack[i] = block
                pack[144 + i, 0:2] = own[i, y, 2:4]
                pack[144 + i, 2:4] = rows[4:6]
                ex[i, y, 0:2] = own[i, y, 4:6]
                ex[i, y, 2:4] = rows[6:8]
        new, old = turn(q_tp, [tp[i, there] for i in at]), [tp[i, here] for i in at]
        for c, i in enumerate(at):
            for y, (pack, rows) in enumerate(by_y(i, old[c], new[c])):
                pack[72 + i, 0:4] = rows[4:8]
                pack[144 + i, 4:6] = rows[2:4]
                ex[i, y, 4:6] = rows[4:6]
        new, old = turn(q_far, joined(far, far_tail, here)), joined(far, far_tail, there)
        for c, i in enumerate(at):
            for y, (pack, rows) in enumerate(by_y(i, new[c], old[c])):
                pack[72 + i, 4:8] = rows[0:4]
                pack[144 + i, 6:8] = rows[4:6]
                ex[i, y, 6:8] = rows[6:8]


VM = pl.BlockSpec(memory_space=pltpu.VMEM)
SM = pl.BlockSpec(memory_space=pltpu.SMEM)


def params(mib):
    return pltpu.CompilerParams(vmem_limit_bytes=mib * 1024 * 1024)


def run_weights(conv_in, bias_in, conv_out, bias_out):
    shapes = [((192, 432), BF16), ((64, 128), F32), ((24, 64), BF16), ((24, 128), F32)]
    return pl.pallas_call(
        weights_kernel,
        out_shape=[jax.ShapeDtypeStruct(*shape) for shape in shapes * 2],
        in_specs=[VM] * 4,
        out_specs=[VM] * 8,
        scratch_shapes=[pltpu.VMEM((512, 256), F32), pltpu.VMEM((128, 128), F32)],
        compiler_params=params(8),
        cost_estimate=pl.CostEstimate(flops=0, bytes_accessed=6_000_000, transcendentals=0),
        name="weights",
    )(conv_in, bias_in, conv_out, bias_out)


def run_unpack(x, rows):
    lengths = (8, 2, 2) if rows else (8,)
    return pl.pallas_call(
        unpack_kernel,
        out_shape=[jax.ShapeDtypeStruct((72, 2, n, 128), F32) for n in lengths],
        in_specs=[VM],
        out_specs=[VM] * len(lengths),
        compiler_params=params(8),
        cost_estimate=pl.CostEstimate(flops=0, bytes_accessed=2_000_000, transcendentals=0),
        name="unpack",
    )(x.reshape(72, 16, 128))


def run_tail(own):
    return pl.pallas_call(
        tail_kernel,
        out_shape=jax.ShapeDtypeStruct((72, 2, 6, 128), F32),
        in_specs=[VM],
        out_specs=VM,
        compiler_params=params(8),
        cost_estimate=pl.CostEstimate(flops=0, bytes_accessed=1_000_000, transcendentals=0),
        name="tail",
    )(own)


def run_traces(mode, ya, *inputs):
    parts = 3 if mode == "wide" else 1
    placed = [pltpu.VMEM((72, 2, 8, 128), F32)] if mode == "single" else []
    return pl.pallas_call(
        functools.partial(trace_kernel, mode),
        out_shape=jax.ShapeDtypeStruct((16 * parts, 16, 128), BF16),
        in_specs=[SM] + [VM] * len(inputs),
        out_specs=VM,
        scratch_shapes=[pltpu.VMEM((256 * parts, 128), F32)] + placed,
        compiler_params=params(10),
        cost_estimate=pl.CostEstimate(flops=8_000_000, bytes_accessed=6_000_000, transcendentals=0),
        name="traces",
    )(ya, *inputs)


def run_staples(mode, ya, *inputs):
    return pl.pallas_call(
        functools.partial(staple_kernel, mode),
        out_shape=jax.ShapeDtypeStruct((24, 18, 8, 128), F32),
        in_specs=[SM] + [VM] * len(inputs),
        out_specs=VM,
        scratch_shapes=[pltpu.VMEM((72, 4, 24, 128), F32)] * 3,
        compiler_params=params(22),
        cost_estimate=pl.CostEstimate(
            flops=20_000_000, bytes_accessed=16_000_000, transcendentals=0
        ),
        name="staples",
    )(ya, *inputs)


def run_final(ya, own, staples, f, f_s, w_in, b_in, w_out, b_out, last):
    weights = [pltpu.VMEM((2, 192, 128), F32)]
    shapes = [(72, 16, 128)] if last else [(72, 2, 8, 128), (36, 8, 128)]
    return pl.pallas_call(
        last_kernel if last else final_kernel,
        out_shape=[jax.ShapeDtypeStruct(shape, F32) for shape in shapes],
        in_specs=[SM] + [VM] * 8,
        out_specs=[VM] * len(shapes),
        scratch_shapes=([pltpu.VMEM((72, 2, 8, 128), F32)] if last else []) + weights,
        compiler_params=params(14),
        cost_estimate=pl.CostEstimate(flops=300_000_000, bytes_accessed=4_000_000, transcendentals=131072),
        name="rotate",
    )(ya, own, staples, f, f_s, w_in, b_in, w_out, b_out)


def run_shift(ya, *arrays):
    block, pack = (72, 2, 8, 128), (216, 8, 128)
    return pl.pallas_call(
        shift_kernel,
        out_shape=[jax.ShapeDtypeStruct(shape, F32) for shape in (block, pack, pack, block)],
        in_specs=[SM] + [VM] * 9,
        out_specs=[VM] * 4,
        compiler_params=params(12),
        cost_estimate=pl.CostEstimate(flops=8_000_000, bytes_accessed=6_000_000, transcendentals=0),
        name="shift",
    )(ya, *arrays)


def step(value, axis, by):
    count = lax.axis_size(axis)
    return lax.ppermute(value, axis, [((i + by) % count, i) for i in range(count)])


def diagonal(value, x_by, t_by):
    n_x, n_t = lax.axis_size("space"), lax.axis_size("tm")
    pairs = [
        ((i + x_by) % n_x * n_t + (k + t_by) % n_t, i * n_t + k)
        for i in range(n_x)
        for k in range(n_t)
    ]
    return lax.ppermute(value, ("space", "tm"), pairs)


def other_time(value, dim, x_by=0):
    if lax.axis_size("tm") == 2:
        return diagonal(value, x_by, 1)
    up = diagonal(lax.slice_in_dim(value, 0, 1, axis=dim), x_by, 1)
    down = diagonal(lax.slice_in_dim(value, 1, 2, axis=dim), x_by, -1)
    return jnp.concatenate([up, down], axis=dim)


def other_rows(value, x_by=0):
    split = value.reshape(value.shape[:-2] + (value.shape[-2] // 2, 2, 128))
    return other_time(split, split.ndim - 2, x_by).reshape(value.shape)


def active_rows(active_blocks):
    index = (lax.axis_index("tm"), lax.axis_index("space"), 2 * lax.axis_index("sub"))
    at = lax.dynamic_slice(active_blocks, (0, 0) + index, active_blocks.shape[:2] + (1, 1, 1))
    return jnp.where(at[:, :, 0, 0, 0] > 0, 0, 1).astype(jnp.int32)


def per_device(gauge_links, active_blocks, conv_in, bias_in, conv_out, bias_out):
    tp_raw = other_time(gauge_links, 2)
    own, first, last = run_unpack(gauge_links, True)
    ya = active_rows(active_blocks)
    weights = run_weights(conv_in, bias_in, conv_out, bias_out)

    right = step(first, "space", 1)
    left = step(last, "space", -1)
    tail = step(run_tail(own), "space", 1)
    own_s = step(own, "sub", 1)
    right, left, ya, weights = lax.optimization_barrier((right, left, ya, weights))
    ya = [ya[0], ya[1]]
    mixed = jnp.concatenate([left[18:36, :, 0:1], right[0:18, :, 1:2]], axis=2)
    co = other_time(mixed, 2)
    h = jnp.concatenate([left, right], axis=2)
    h_s = step(h, "sub", 1)
    (tp,) = run_unpack(tp_raw, False)
    tr = run_traces("single", ya[0], own, own_s, tp, right).reshape(2, 4, 2, 16, 128)
    far = other_rows(right)
    full = other_traces(tr)
    full, co, far, tail = lax.optimization_barrier((full, co, far, tail))
    far_tail = other_rows(tail)
    tp_s, co_s = step(tp, "sub", 1), step(co, "sub", 1)
    f, staples = rim(
        full, lambda: run_staples("single", ya[0], own, own_s, tp, tp_s, h, h_s, co, co_s)
    )
    f_s = step(f, "sub", 1)
    own, q = run_final(ya[0], own, staples, f, f_s, *weights[:4], False)

    q_tp = other_rows(q)
    q_far = other_rows(q, 1)
    q_next = step(q, "space", 1)
    own, pack_0, pack_1, ex = run_shift(
        ya[0], own, right, tail, tp, far, far_tail, q_next, q_tp, q_far
    )

    other_0, other_1 = step(pack_0, "sub", 1), step(pack_1, "sub", 1)

    def staples_1():
        return run_staples("packs", ya[1], pack_0, pack_1, other_0, other_1)

    if lax.axis_size("tm") == 2:
        f = run_traces("wide", ya[1], pack_0, pack_1, other_0, ex).reshape(2, 6, 4, 16, 128)
        staples = staples_1()
    else:
        tr = run_traces("packs", ya[1], pack_0, pack_1, other_0, ex).reshape(2, 4, 2, 16, 128)
        f, staples = rim(other_traces(tr), staples_1)
    f_s = step(f, "sub", 1)
    (out,) = run_final(ya[1], own, staples, f, f_s, *weights[4:], True)
    return out.reshape(4, 18, 2, 4, 2, 128)


def other_traces(tr):
    times = other_time(tr, 2)
    return jnp.concatenate([times[:, :, 1:2], tr, times[:, :, 0:1]], axis=2)


def rim(full, meanwhile):
    before = step(full[:, 3:4], "space", -1)
    after = step(full[:, 0:1], "space", 1)
    other = meanwhile()
    before, after, other = lax.optimization_barrier((before, after, other))
    return jnp.concatenate([before, full, after], axis=1), other


def solution(mesh):
    placed = (
        P(None, None, ("grp", "tm"), "space", "sub", None),
        P("grp", None, None, None, None),
        P(),
        P(),
        P(),
        P(),
    )
    return jax.shard_map(
        per_device,
        mesh=mesh,
        in_specs=placed,
        out_specs=P(None, None, ("grp", "tm"), "space", "sub", None),
        check_vma=False,
    )
```

```python
import functools

import jax
import jax.numpy as jnp
from jax import lax
from jax.experimental import pallas as pl
from jax.experimental.pallas import tpu as pltpu
from jax.sharding import PartitionSpec as P

PAIRS = ((0, 1), (0, 2), (0, 3), (1, 2), (1, 3), (2, 3))
HALVES = (((3, 4, 5), (0, 1, 2)), ((0, 2, 4), (1, 3, 5)))
F32 = jnp.float32
BF16 = jnp.bfloat16
BASE = 8


def mm(a, b, a_dag=False, b_dag=False):
    out_re, out_im = [], []
    for i in range(3):
        row_re, row_im = [], []
        for j in range(3):
            re = im = None
            for k in range(3):
                ar, ai = (a[0][k][i], a[1][k][i]) if a_dag else (a[0][i][k], a[1][i][k])
                br, bi = (b[0][j][k], b[1][j][k]) if b_dag else (b[0][k][j], b[1][k][j])
                if a_dag:
                    r, m = ar * br + ai * bi, ar * bi - ai * br
                elif b_dag:
                    r, m = ar * br + ai * bi, ai * br - ar * bi
                else:
                    r, m = ar * br - ai * bi, ar * bi + ai * br
                re = r if re is None else re + r
                im = m if im is None else im + m
            row_re.append(re)
            row_im.append(im)
        out_re.append(row_re)
        out_im.append(row_im)
    return out_re, out_im


def as_matrix(parts):
    return (
        [[parts[3 * i + j] for j in range(3)] for i in range(3)],
        [[parts[9 + 3 * i + j] for j in range(3)] for i in range(3)],
    )


def flat(matrix):
    return [matrix[0][i][j] for i in range(3) for j in range(3)] + [
        matrix[1][i][j] for i in range(3) for j in range(3)
    ]


def cmul(a, b):
    return a[0] * b[0] - a[1] * b[1], a[0] * b[1] + a[1] * b[0]


def zroll(value, step):
    return pltpu.roll(value, (-step) % value.shape[-1], value.ndim - 1)


def trace_kernel(mode, planes, merge, ya, *refs):
    if merge:
        others, refs = refs[0], refs[1:]
    if mode == "single":
        own, own_s, tp, right, *outs, placed = refs

        def place(i, _):
            for y in range(2):
                placed[i, y, 6:8] = right[i, y]
            return 0

        lax.fori_loop(0, 72, place, 0, unroll=8)
    else:
        packs, ex, outs = refs[:3], refs[3], refs[4:]
    trs = outs[-1]
    wide = mode == "wide"
    parts = 3 if wide else 1
    count = 16 * parts
    row_of = lax.broadcasted_iota(jnp.int32, (8, 128), 0)
    even = row_of % 2 == 0

    def links(part, y, i):
        if mode == "single":
            return own_s[i, 0] if y == 2 else (own, tp)[part][i, y]
        return packs[y][72 * part + i]

    def later(part, y, i):
        o = links(part, y, i)
        t = pltpu.roll(o, 4, 0) if part == 2 else links(1 - part, y, i)
        return jnp.where(even, pltpu.roll(o, 7, 0), pltpu.roll(t, 1, 0))

    def right_of(part, y, i):
        if part == 2:
            return ex[i, y]
        if mode == "single":
            after = placed[i, y]
        else:
            after = links(2, y, i)
            after = pltpu.roll(after, 4, 0) if part == 0 else after
        return jnp.where(row_of < 6, pltpu.roll(links(part, y, i), 6, 0), after)

    trs[6 * count :] = jnp.zeros((2 * count, 128), F32)
    for part in range(parts):
        inner = jnp.where(row_of >= 6, 1, 0)
        leaves = (row_of % 2, 1 - row_of // 2 % 2 if part == 2 else inner, 1, 0)
        flip = jnp.where(row_of < 4, 1, 0) if part == 2 else part
        for y in range(2):
            active = [jnp.where(ya[m] == y, 1, 0) ^ flip for m in range(4)]

            def look(d, step):
                at = range(18 * d, 18 * d + 18)
                if step == 0:
                    return as_matrix([later(part, y, i) for i in at])
                if step == 1:
                    return as_matrix([right_of(part, y, i) for i in at])
                if step == 2:
                    return as_matrix([links(part, y + 1, i) for i in at])
                values = [links(part, y, i) for i in at]
                return as_matrix([zroll(v, 1) for v in values] if step == 3 else values)

            for p, (m, n) in enumerate(PAIRS[plane] for plane in planes):
                a = flat(mm(look(m, None), look(n, m)))
                b = flat(mm(look(n, None), look(m, n)))
                re = im = None
                for k in range(9):
                    r = a[k] * b[k] + a[9 + k] * b[9 + k]
                    q = a[9 + k] * b[k] - a[k] * b[9 + k]
                    re = r if re is None else re + r
                    im = q if im is None else im + q
                moved = (active[n] ^ leaves[m]) | (active[m] ^ leaves[n]) | active[m] | active[n]
                frozen = jnp.broadcast_to(moved, (8, 128)) == 0
                for k, value in enumerate((re, im)):
                    row = (2 * p + k) * count + 16 * part + 8 * y
                    trs[row : row + 8] = jnp.where(frozen, value * (1.0 / 3.0), 0.0)
    for r in range(count if merge else 0):
        place = r
        if wide:
            part, y, row = r // 16, r // 8 % 2, r % 8
            if part < 2:
                partner, x = part, 1 + row // 2
            else:
                partner, x = row // 4, (0, 5)[row // 2 % 2]
            t = (3, 0)[row % 2] if partner else 1 + row % 2
            place = (6 * y + x) * 4 + t
        halves = [ref[pl.ds(r, 8, stride=count), :] for ref in (others, trs)]
        outs[0][place] = jnp.concatenate(halves, axis=0).astype(BF16)


def staple_kernel(mode, ya, *refs):
    inputs, (out, v0, vup, vdn) = refs[:-4], refs[-4:]
    even = lax.broadcasted_iota(jnp.int32, (8, 128), 0) % 2 == 0
    places = ((1, 1), (0, 0), (0, 1), (1, 0))
    if mode == "single":
        own, own_s, tp, tp_s, h, h_s, co, co_s = inputs

    def prep(i, _):
        for y, (other, at) in enumerate(places):
            if mode == "single":
                o, t = (own, own_s)[other][i, at], (tp, tp_s)[other][i, at]
                hh = (h, h_s)[other][i, at]
            else:
                pack = inputs[2 * other + at]
                o, t, hh = pack[i], pack[72 + i], pack[144 + i]
            v0[i, y, BASE : BASE + 8] = o
            v0[i, y, BASE - 2 : BASE] = hh[0:2]
            v0[i, y, BASE + 8 : BASE + 10] = hh[2:4]
            vup[i, y, BASE : BASE + 8] = jnp.where(even, pltpu.roll(o, 7, 0), pltpu.roll(t, 1, 0))
            vdn[i, y, BASE : BASE + 8] = jnp.where(even, pltpu.roll(t, 7, 0), pltpu.roll(o, 1, 0))
        return 0

    lax.fori_loop(0, 72, prep, 0, unroll=4)

    def corner(c, _):
        for y, (other, at) in enumerate(places):
            if mode == "single":
                hh, cc = (h, h_s)[other], (co, co_s)[other]
                x_links = hh[18 + c, at, 1:2], cc[c, at, 0:1]
                t_links = cc[c, at, 1:2], hh[c, at, 2:3]
            else:
                pack = inputs[2 * other + at]
                x_links = pack[162 + c, 1:2], pack[162 + c, 4:5]
                t_links = pack[144 + c, 7:8], pack[144 + c, 2:3]
            vup[18 + c, y, BASE - 2 : BASE - 1] = x_links[0]
            vup[18 + c, y, BASE - 1 : BASE] = x_links[1]
            vdn[c, y, BASE + 8 : BASE + 9] = t_links[0]
            vdn[c, y, BASE + 9 : BASE + 10] = t_links[1]
        return 0

    lax.fori_loop(0, 18, corner, 0, unroll=2)

    for m in range(4):
        yy = ya[m] + 1

        def look(d, offset):
            source = {0: v0, 1: vup, -1: vdn}[offset[0]]
            row = BASE + 2 * offset[1]
            parts = [source[18 * d + c, yy + offset[2], row : row + 8] for c in range(18)]
            if offset[3] != 0:
                parts = [zroll(p, offset[3]) for p in parts]
            return as_matrix(parts)

        zero = (0, 0, 0, 0)
        others = [n for n in range(4) if n != m]
        for j, n in enumerate(others):
            step_m = tuple(int(k == m) for k in range(4))
            step_n = tuple(int(k == n) for k in range(4))
            back_n = tuple(-k for k in step_n)
            corner_mn = tuple(a - b for a, b in zip(step_m, step_n))
            up = mm(look(n, step_m), mm(look(n, zero), look(m, step_n)), b_dag=True)
            for c, value in enumerate(flat(up)):
                out[6 * m + 2 * j, c] = value
            down = mm(mm(look(m, back_n), look(n, corner_mn)), look(n, back_n), a_dag=True)
            for c, value in enumerate(flat(down)):
                out[6 * m + 2 * j + 1, c] = value


def even_rows():
    return lax.broadcasted_iota(jnp.int32, (8, 128), 0) % 2 == 0


def exchanged(a, b, even):
    return jnp.where(even, a, pltpu.roll(b, 1, 0)), jnp.where(even, pltpu.roll(a, 7, 0), b)


def unpack_kernel(x, own, *rows):
    even = even_rows()

    def body(i, _):
        own[i, 0], own[i, 1] = exchanged(x[i, 0:8], x[i, 8:16], even)
        if rows:
            for y in range(2):
                for t in range(2):
                    at = 8 * t + y
                    rows[0][i, y, t : t + 1] = x[i, at : at + 1]
                    rows[1][i, y, t : t + 1] = x[i, at + 6 : at + 7]
        return 0

    lax.fori_loop(0, 72, body, 0, unroll=8)


def tail_kernel(own, tail):
    def body(i, _):
        for y in range(2):
            tail[i, y] = own[i, y, 2:8]
        return 0

    lax.fori_loop(0, 72, body, 0, unroll=8)


def weights_kernel(conv_in, bias_in, conv_out, bias_out, *refs):
    outs, big, small = refs[:8], refs[8], refs[9]
    big[...] = jnp.zeros_like(big)
    small[...] = jnp.zeros_like(small)
    for layer in range(2):
        w_in, b_in, w_out, b_out = outs[4 * layer : 4 * layer + 4]
        for k in range(27):
            taps = [conv_in[layer, 3 * k + z].astype(F32) for z in range(3)]
            taps = jnp.concatenate(taps, axis=1)
            for half, planes in enumerate(HALVES[layer]):
                for a, plane in enumerate(planes):
                    at = 16 * k + 8 * half + 2 * a
                    big[at : at + 2, 0:192] = taps[2 * plane : 2 * plane + 2]
        w_in[...] = jnp.transpose(big[...])[0:192, 0:432].astype(BF16)
        small[0:64, 0:24] = conv_out[layer].astype(F32)
        w_out[...] = jnp.transpose(small[...])[0:24, 0:64].astype(BF16)
        small[:, 0:64] = jnp.broadcast_to(bias_in[layer : layer + 1], (128, 64))
        b_in[...] = jnp.transpose(small[...])[0:64]
        small[:, 0:24] = jnp.broadcast_to(bias_out[layer : layer + 1], (128, 24))
        b_out[...] = jnp.transpose(small[...])[0:24]


def last_kernel(ya, own, staples, f, f_s, w_in, b_in, w_out, b_out, out, packed, wts, sems):
    even = even_rows()

    def store(i, y, value, old):
        at_0 = y == 0
        tiles = jnp.where(at_0, value, old), jnp.where(at_0, old, value)
        packed[i, 0:8], packed[i, 8:16] = exchanged(*tiles, even)

    def copy(m):
        part = slice(18 * m, 18 * m + 18)
        return pltpu.make_async_copy(packed.at[part], out.at[part], sems.at[m])

    update(
        ya, own, staples, f, f_s, w_in, b_in, w_out, b_out, wts, store,
        done=lambda m: copy(m).start(),
    )
    for m in range(4):
        copy(m).wait()


def final_kernel(ya, own, staples, f, f_s, w_in, b_in, w_out, b_out, out, sent, wts):
    def store(i, y, value, old):
        out[i, y] = value
        out[i, 1 - y] = old

    update(ya, own, staples, f, f_s, w_in, b_in, w_out, b_out, wts, store, sent)


def update(
    ya, own, staples, f, f_s, w_in, b_in, w_out, b_out, wts, store, sent=None, done=None
):
    places = ((1, 1), (0, 0), (0, 1), (1, 0))
    sites = [(y, r // 2, r % 2) for y in range(2) for r in range(8)]
    columns = []
    for y, x, t in sites:
        tiles = []
        for a in range(3):
            for b in range(3):
                for c in range(3):
                    other, at = places[y + c]
                    tiles.append((f, f_s)[other][at, x + b, t + a])
        columns.append(jnp.concatenate(tiles, axis=0))
    g = jnp.dot(w_in[...], jnp.concatenate(columns, axis=1), preferred_element_type=F32)
    hidden = []
    for k in range(16):
        lanes = slice(128 * k, 128 * k + 128)
        part = zroll(g[0:64, lanes], -1) + g[64:128, lanes] + zroll(g[128:192, lanes], 1)
        hidden.append(jnp.tanh(part + b_in[...]).astype(BF16))
    weights = jnp.dot(w_out[...], jnp.concatenate(hidden, axis=1), preferred_element_type=F32)
    for k in range(16):
        row = 24 * (k % 8)
        wts[k // 8, row : row + 24] = weights[:, 128 * k : 128 * k + 128] + b_out[...]

    for m in range(4):
        y = ya[m]
        link = as_matrix([own[18 * m + c, y] for c in range(18)])
        total = None
        for k in range(6 * m, 6 * m + 6):
            w = wts[y, pl.ds(k, 8, stride=24), :]
            term = [w * staples[k, c] for c in range(18)]
            total = term if total is None else [a + b for a, b in zip(total, term)]
        are, aim = mm(link, as_matrix(total))
        trace_im = (aim[0][0] + aim[1][1] + aim[2][2]) * (1.0 / 3.0)
        low = []
        for i, k in ((0, 1), (0, 2), (1, 2)):
            low.append(-0.25 * (are[i][k] - are[k][i]))
            low.append(-0.25 * (aim[i][k] + aim[k][i]))
        low += [-0.5 * (aim[i][i] - trace_im) for i in range(3)]
        if sent is not None:
            for c in range(9):
                sent[9 * m + c] = low[c]
        for c, value in enumerate(rotated(low, link)):
            store(18 * m + c, y, value, own[18 * m + c, 1 - y])
        if done is not None:
            done(m)


def rotated(low, link):
    one = jnp.ones_like(low[0])
    full = [[None] * 3 for _ in range(3)]
    for i in range(3):
        full[i][i] = (one, low[6 + i])
    for at, (i, k) in enumerate(((0, 1), (0, 2), (1, 2))):
        re, im = low[2 * at], low[2 * at + 1]
        full[i][k] = (re, im)
        full[k][i] = (-re, im)
    adj_re, adj_im = [], []
    for i in range(3):
        row_re, row_im = [], []
        for j in range(3):
            first = cmul(full[(j + 1) % 3][(i + 1) % 3], full[(j + 2) % 3][(i + 2) % 3])
            second = cmul(full[(j + 1) % 3][(i + 2) % 3], full[(j + 2) % 3][(i + 1) % 3])
            row_re.append(first[0] - second[0])
            row_im.append(first[1] - second[1])
        adj_re.append(row_re)
        adj_im.append(row_im)
    det_re = det_im = None
    for k in range(3):
        product = cmul(full[0][k], (adj_re[k][0], adj_im[k][0]))
        det_re = product[0] if det_re is None else det_re + product[0]
        det_im = product[1] if det_im is None else det_im + product[1]
    twice = 2.0 / (det_re * det_re + det_im * det_im)
    scale_re = det_re * twice
    scale_im = -det_im * twice
    turned = flat(mm((adj_re, adj_im), link))
    current = flat(link)
    real, imag = [], []
    for c in range(9):
        re, im = cmul((turned[c], turned[9 + c]), (scale_re, scale_im))
        real.append(re - current[c])
        imag.append(im - current[9 + c])
    return real + imag


def shift_kernel(
    ya, own, right, tail, tp, far, far_tail, q_next, q_tp, q_far, own_o, pack_0, pack_1, ex
):
    for m in range(4):
        here = ya[m]
        there = 1 - here
        at = [18 * m + c for c in range(18)]

        def turn(q, links):
            return rotated([q[9 * m + c] for c in range(9)], as_matrix(links))

        def joined(one, more, y):
            return [jnp.concatenate([one[i, y], more[i, y]], axis=0) for i in at]

        at_0 = here == 0

        def by_y(i, if_here, if_there):
            return (
                (pack_0, jnp.where(at_0, if_here, if_there)),
                (pack_1, jnp.where(at_0, if_there, if_here)),
            )

        new, old = turn(q_next, joined(right, tail, there)), joined(right, tail, here)
        for c, i in enumerate(at):
            for y, (pack, rows) in enumerate(by_y(i, old[c], new[c])):
                block = jnp.concatenate([own[i, y, 4:8], rows[0:4]], axis=0)
                own_o[i, y] = block
                pack[i] = block
                pack[144 + i, 0:2] = own[i, y, 2:4]
                pack[144 + i, 2:4] = rows[4:6]
                ex[i, y, 0:2] = own[i, y, 4:6]
                ex[i, y, 2:4] = rows[6:8]
        new, old = turn(q_tp, [tp[i, there] for i in at]), [tp[i, here] for i in at]
        for c, i in enumerate(at):
            for y, (pack, rows) in enumerate(by_y(i, old[c], new[c])):
                pack[72 + i, 0:4] = rows[4:8]
                pack[144 + i, 4:6] = rows[2:4]
                ex[i, y, 4:6] = rows[4:6]
        new, old = turn(q_far, joined(far, far_tail, here)), joined(far, far_tail, there)
        for c, i in enumerate(at):
            for y, (pack, rows) in enumerate(by_y(i, new[c], old[c])):
                pack[72 + i, 4:8] = rows[0:4]
                pack[144 + i, 6:8] = rows[4:6]
                ex[i, y, 6:8] = rows[6:8]


VM = pl.BlockSpec(memory_space=pltpu.VMEM)
SM = pl.BlockSpec(memory_space=pltpu.SMEM)


def params(mib):
    return pltpu.CompilerParams(vmem_limit_bytes=mib * 1024 * 1024)


def run_weights(conv_in, bias_in, conv_out, bias_out):
    shapes = [((192, 432), BF16), ((64, 128), F32), ((24, 64), BF16), ((24, 128), F32)]
    return pl.pallas_call(
        weights_kernel,
        out_shape=[jax.ShapeDtypeStruct(*shape) for shape in shapes * 2],
        in_specs=[VM] * 4,
        out_specs=[VM] * 8,
        scratch_shapes=[pltpu.VMEM((512, 256), F32), pltpu.VMEM((128, 128), F32)],
        compiler_params=params(8),
        cost_estimate=pl.CostEstimate(flops=0, bytes_accessed=6_000_000, transcendentals=0),
        name="weights",
    )(conv_in, bias_in, conv_out, bias_out)


def run_unpack(x, rows):
    lengths = (8, 2, 2) if rows else (8,)
    return pl.pallas_call(
        unpack_kernel,
        out_shape=[jax.ShapeDtypeStruct((72, 2, n, 128), F32) for n in lengths],
        in_specs=[VM],
        out_specs=[VM] * len(lengths),
        compiler_params=params(8),
        cost_estimate=pl.CostEstimate(flops=0, bytes_accessed=2_000_000, transcendentals=0),
        name="unpack",
    )(x.reshape(72, 16, 128))


def run_tail(own):
    return pl.pallas_call(
        tail_kernel,
        out_shape=jax.ShapeDtypeStruct((72, 2, 6, 128), F32),
        in_specs=[VM],
        out_specs=VM,
        compiler_params=params(8),
        cost_estimate=pl.CostEstimate(flops=0, bytes_accessed=1_000_000, transcendentals=0),
        name="tail",
    )(own)


def run_traces(mode, half, ya, *inputs):
    rows = (16 if mode == "single" else 48 if mode == "wide" else 16)
    channels = (8 * rows, 128)
    placed = [pltpu.VMEM((72, 2, 8, 128), F32)] if mode == "single" else []
    shape = ((rows, 16, 128), BF16) if half else (channels, F32)
    return pl.pallas_call(
        functools.partial(trace_kernel, mode, HALVES[mode != "single"][half], half == 1),
        out_shape=jax.ShapeDtypeStruct(*shape),
        in_specs=[SM] + [VM] * len(inputs),
        out_specs=VM,
        scratch_shapes=([pltpu.VMEM(channels, F32)] if half else []) + placed,
        compiler_params=params(10),
        cost_estimate=pl.CostEstimate(flops=4_000_000, bytes_accessed=4_000_000, transcendentals=0),
        name="traces",
    )(ya, *inputs)


def run_staples(mode, ya, *inputs):
    return pl.pallas_call(
        functools.partial(staple_kernel, mode),
        out_shape=jax.ShapeDtypeStruct((24, 18, 8, 128), F32),
        in_specs=[SM] + [VM] * len(inputs),
        out_specs=VM,
        scratch_shapes=[pltpu.VMEM((72, 4, 24, 128), F32)] * 3,
        compiler_params=params(22),
        cost_estimate=pl.CostEstimate(
            flops=20_000_000, bytes_accessed=16_000_000, transcendentals=0
        ),
        name="staples",
    )(ya, *inputs)


def run_final(ya, own, staples, f, f_s, w_in, b_in, w_out, b_out, last):
    weights = [pltpu.VMEM((2, 192, 128), F32)]
    shapes = [(72, 16, 128)] if last else [(72, 2, 8, 128), (36, 8, 128)]
    return pl.pallas_call(
        last_kernel if last else final_kernel,
        out_shape=[jax.ShapeDtypeStruct(shape, F32) for shape in shapes],
        in_specs=[SM] + [VM] * 8,
        out_specs=[pl.BlockSpec(memory_space=pl.ANY) if last else VM] + [VM] * (len(shapes) - 1),
        scratch_shapes=(
            [pltpu.VMEM((72, 16, 128), F32)] + weights + [pltpu.SemaphoreType.DMA((4,))]
            if last
            else weights
        ),
        compiler_params=params(14),
        cost_estimate=pl.CostEstimate(flops=300_000_000, bytes_accessed=4_000_000, transcendentals=131072),
        name="rotate",
    )(ya, own, staples, f, f_s, w_in, b_in, w_out, b_out)


def run_shift(ya, *arrays):
    block, pack = (72, 2, 8, 128), (216, 8, 128)
    return pl.pallas_call(
        shift_kernel,
        out_shape=[jax.ShapeDtypeStruct(shape, F32) for shape in (block, pack, pack, block)],
        in_specs=[SM] + [VM] * 9,
        out_specs=[VM] * 4,
        compiler_params=params(12),
        cost_estimate=pl.CostEstimate(flops=8_000_000, bytes_accessed=6_000_000, transcendentals=0),
        name="shift",
    )(ya, *arrays)


def step(value, axis, by):
    count = lax.axis_size(axis)
    return lax.ppermute(value, axis, [((i + by) % count, i) for i in range(count)])


def diagonal(value, x_by, t_by):
    n_x, n_t = lax.axis_size("space"), lax.axis_size("tm")
    pairs = [
        ((i + x_by) % n_x * n_t + (k + t_by) % n_t, i * n_t + k)
        for i in range(n_x)
        for k in range(n_t)
    ]
    return lax.ppermute(value, ("space", "tm"), pairs)


def other_time(value, dim, x_by=0):
    if lax.axis_size("tm") == 2:
        return diagonal(value, x_by, 1)
    up = diagonal(lax.slice_in_dim(value, 0, 1, axis=dim), x_by, 1)
    down = diagonal(lax.slice_in_dim(value, 1, 2, axis=dim), x_by, -1)
    return jnp.concatenate([up, down], axis=dim)


def other_rows(value, x_by=0):
    split = value.reshape(value.shape[:-2] + (value.shape[-2] // 2, 2, 128))
    return other_time(split, split.ndim - 2, x_by).reshape(value.shape)


def active_rows(active_blocks):
    index = (lax.axis_index("tm"), lax.axis_index("space"), 2 * lax.axis_index("sub"))
    at = lax.dynamic_slice(active_blocks, (0, 0) + index, active_blocks.shape[:2] + (1, 1, 1))
    return jnp.where(at[:, :, 0, 0, 0] > 0, 0, 1).astype(jnp.int32)


def per_device(gauge_links, active_blocks, conv_in, bias_in, conv_out, bias_out):
    tp_raw = other_time(gauge_links, 2)
    own, first, last = run_unpack(gauge_links, True)
    ya = active_rows(active_blocks)
    weights = run_weights(conv_in, bias_in, conv_out, bias_out)

    right = step(first, "space", 1)
    left = step(last, "space", -1)
    tail = step(run_tail(own), "space", 1)
    own_s = step(own, "sub", 1)
    right, left, ya, weights = lax.optimization_barrier((right, left, ya, weights))
    ya = [ya[0], ya[1]]
    mixed = jnp.concatenate([left[18:36, :, 0:1], right[0:18, :, 1:2]], axis=2)
    co = other_time(mixed, 2)
    h = jnp.concatenate([left, right], axis=2)
    h_s = step(h, "sub", 1)
    (tp,) = run_unpack(tp_raw, False)
    half = run_traces("single", 0, ya[0], own, own_s, own, right)
    tr = run_traces("single", 1, ya[0], half, own, own_s, tp, right).reshape(2, 4, 2, 16, 128)
    far = other_rows(right)
    full = other_traces(tr)
    full, co, far, tail = lax.optimization_barrier((full, co, far, tail))
    far_tail = other_rows(tail)
    tp_s, co_s = step(tp, "sub", 1), step(co, "sub", 1)
    f, staples = rim(
        full, lambda: run_staples("single", ya[0], own, own_s, tp, tp_s, h, h_s, co, co_s)
    )
    f_s = step(f, "sub", 1)
    own, q = run_final(ya[0], own, staples, f, f_s, *weights[:4], False)

    q_tp = other_rows(q)
    q_far = other_rows(q, 1)
    q_next = step(q, "space", 1)
    own, pack_0, pack_1, ex = run_shift(
        ya[0], own, right, tail, tp, far, far_tail, q_next, q_tp, q_far
    )

    other_0, other_1 = step(pack_0, "sub", 1), step(pack_1, "sub", 1)

    def staples_1():
        return run_staples("packs", ya[1], pack_0, pack_1, other_0, other_1)

    mode = "wide" if lax.axis_size("tm") == 2 else "packs"
    half = run_traces(mode, 0, ya[1], pack_0, pack_1, pack_0, ex)
    tr = run_traces(mode, 1, ya[1], half, pack_0, pack_1, other_0, ex)
    if mode == "wide":
        f = tr.reshape(2, 6, 4, 16, 128)
        staples = staples_1()
    else:
        f, staples = rim(other_traces(tr.reshape(2, 4, 2, 16, 128)), staples_1)
    f_s = step(f, "sub", 1)
    (out,) = run_final(ya[1], own, staples, f, f_s, *weights[4:], True)
    return out.reshape(4, 18, 2, 4, 2, 128)


def other_traces(tr):
    times = other_time(tr, 2)
    return jnp.concatenate([times[:, :, 1:2], tr, times[:, :, 0:1]], axis=2)


def rim(full, meanwhile):
    before = step(full[:, 3:4], "space", -1)
    after = step(full[:, 0:1], "space", 1)
    other = meanwhile()
    before, after, other = lax.optimization_barrier((before, after, other))
    return jnp.concatenate([before, full, after], axis=1), other


def solution(mesh):
    placed = (
        P(None, None, ("grp", "tm"), "space", "sub", None),
        P("grp", None, None, None, None),
        P(),
        P(),
        P(),
        P(),
    )
    return jax.shard_map(
        per_device,
        mesh=mesh,
        in_specs=placed,
        out_specs=P(None, None, ("grp", "tm"), "space", "sub", None),
        check_vma=False,
    )
```

```python
import functools

import jax
import jax.numpy as jnp
from jax import lax
from jax.experimental import pallas as pl
from jax.experimental.pallas import tpu as pltpu
from jax.sharding import PartitionSpec as P

PAIRS = ((0, 1), (0, 2), (0, 3), (1, 2), (1, 3), (2, 3))
HALVES = (((3, 4, 5), (0, 1, 2)), ((0, 2, 4), (1, 3, 5)))
F32 = jnp.float32
BF16 = jnp.bfloat16
BASE = 8


def mm(a, b, a_dag=False, b_dag=False):
    out_re, out_im = [], []
    for i in range(3):
        row_re, row_im = [], []
        for j in range(3):
            re = im = None
            for k in range(3):
                ar, ai = (a[0][k][i], a[1][k][i]) if a_dag else (a[0][i][k], a[1][i][k])
                br, bi = (b[0][j][k], b[1][j][k]) if b_dag else (b[0][k][j], b[1][k][j])
                if a_dag:
                    r, m = ar * br + ai * bi, ar * bi - ai * br
                elif b_dag:
                    r, m = ar * br + ai * bi, ai * br - ar * bi
                else:
                    r, m = ar * br - ai * bi, ar * bi + ai * br
                re = r if re is None else re + r
                im = m if im is None else im + m
            row_re.append(re)
            row_im.append(im)
        out_re.append(row_re)
        out_im.append(row_im)
    return out_re, out_im


def as_matrix(parts):
    return (
        [[parts[3 * i + j] for j in range(3)] for i in range(3)],
        [[parts[9 + 3 * i + j] for j in range(3)] for i in range(3)],
    )


def flat(matrix):
    return [matrix[0][i][j] for i in range(3) for j in range(3)] + [
        matrix[1][i][j] for i in range(3) for j in range(3)
    ]


def cmul(a, b):
    return a[0] * b[0] - a[1] * b[1], a[0] * b[1] + a[1] * b[0]


def zroll(value, step):
    return pltpu.roll(value, (-step) % value.shape[-1], value.ndim - 1)


def trace_kernel(mode, planes, merge, ya, *refs):
    whole = len(planes) == 6
    if merge and not whole:
        others, refs = refs[0], refs[1:]
    if mode == "single":
        own, own_s, tp, right, *outs, placed = refs

        def place(i, _):
            for y in range(2):
                placed[i, y, 6:8] = right[i, y]
            return 0

        lax.fori_loop(0, 72, place, 0, unroll=8)
    else:
        packs, ex, outs = refs[:3], refs[3], refs[4:]
    trs = outs[-1]
    wide = mode == "wide"
    parts = 3 if wide else 1
    count = 16 * parts
    row_of = lax.broadcasted_iota(jnp.int32, (8, 128), 0)
    even = row_of % 2 == 0

    def links(part, y, i):
        if mode == "single":
            return own_s[i, 0] if y == 2 else (own, tp)[part][i, y]
        return packs[y][72 * part + i]

    def later(part, y, i):
        o = links(part, y, i)
        t = pltpu.roll(o, 4, 0) if part == 2 else links(1 - part, y, i)
        return jnp.where(even, pltpu.roll(o, 7, 0), pltpu.roll(t, 1, 0))

    def right_of(part, y, i):
        if part == 2:
            return ex[i, y]
        if mode == "single":
            after = placed[i, y]
        else:
            after = links(2, y, i)
            after = pltpu.roll(after, 4, 0) if part == 0 else after
        return jnp.where(row_of < 6, pltpu.roll(links(part, y, i), 6, 0), after)

    for group in range(2 if whole else 1):
        first = (8 * group + 6) * count
        trs[first : first + 2 * count] = jnp.zeros((2 * count, 128), F32)
    for part in range(parts):
        inner = jnp.where(row_of >= 6, 1, 0)
        leaves = (row_of % 2, 1 - row_of // 2 % 2 if part == 2 else inner, 1, 0)
        flip = jnp.where(row_of < 4, 1, 0) if part == 2 else part
        for y in range(2):
            active = [jnp.where(ya[m] == y, 1, 0) ^ flip for m in range(4)]

            def look(d, step):
                at = range(18 * d, 18 * d + 18)
                if step == 0:
                    return as_matrix([later(part, y, i) for i in at])
                if step == 1:
                    return as_matrix([right_of(part, y, i) for i in at])
                if step == 2:
                    return as_matrix([links(part, y + 1, i) for i in at])
                values = [links(part, y, i) for i in at]
                return as_matrix([zroll(v, 1) for v in values] if step == 3 else values)

            for p, (m, n) in enumerate(PAIRS[plane] for plane in planes):
                a = flat(mm(look(m, None), look(n, m)))
                b = flat(mm(look(n, None), look(m, n)))
                re = im = None
                for k in range(9):
                    r = a[k] * b[k] + a[9 + k] * b[9 + k]
                    q = a[9 + k] * b[k] - a[k] * b[9 + k]
                    re = r if re is None else re + r
                    im = q if im is None else im + q
                moved = (active[n] ^ leaves[m]) | (active[m] ^ leaves[n]) | active[m] | active[n]
                frozen = jnp.broadcast_to(moved, (8, 128)) == 0
                for k, value in enumerate((re, im)):
                    row = (2 * p + k + 2 * (p // 3)) * count + 16 * part + 8 * y
                    trs[row : row + 8] = jnp.where(frozen, value * (1.0 / 3.0), 0.0)
    for r in range(count if merge else 0):
        place = r
        if wide:
            part, y, row = r // 16, r // 8 % 2, r % 8
            if part < 2:
                partner, x = part, 1 + row // 2
            else:
                partner, x = row // 4, (0, 5)[row // 2 % 2]
            t = (3, 0)[row % 2] if partner else 1 + row % 2
            place = (6 * y + x) * 4 + t
        if whole:
            channels = trs[pl.ds(r, 16, stride=count), :]
        else:
            halves = [ref[pl.ds(r, 8, stride=count), :] for ref in (others, trs)]
            channels = jnp.concatenate(halves, axis=0)
        outs[0][place] = channels.astype(BF16)


def staple_kernel(mode, ya, *refs):
    inputs, (out, v0, vup, vdn) = refs[:-4], refs[-4:]
    even = lax.broadcasted_iota(jnp.int32, (8, 128), 0) % 2 == 0
    places = ((1, 1), (0, 0), (0, 1), (1, 0))
    if mode == "single":
        own, own_s, tp, tp_s, h, h_s, co, co_s = inputs

    def prep(i, _):
        for y, (other, at) in enumerate(places):
            if mode == "single":
                o, t = (own, own_s)[other][i, at], (tp, tp_s)[other][i, at]
                hh = (h, h_s)[other][i, at]
            else:
                pack = inputs[2 * other + at]
                o, t, hh = pack[i], pack[72 + i], pack[144 + i]
            v0[i, y, BASE : BASE + 8] = o
            v0[i, y, BASE - 2 : BASE] = hh[0:2]
            v0[i, y, BASE + 8 : BASE + 10] = hh[2:4]
            if y < 3:
                vup[i, y, BASE : BASE + 8] = jnp.where(
                    even, pltpu.roll(o, 7, 0), pltpu.roll(t, 1, 0)
                )
            if y > 0:
                vdn[i, y, BASE : BASE + 8] = jnp.where(
                    even, pltpu.roll(t, 7, 0), pltpu.roll(o, 1, 0)
                )
        return 0

    lax.fori_loop(0, 72, prep, 0, unroll=4)

    def corner(c, _):
        for y, (other, at) in enumerate(places):
            if mode == "single":
                hh, cc = (h, h_s)[other], (co, co_s)[other]
                x_links = hh[18 + c, at, 1:2], cc[c, at, 0:1]
                t_links = cc[c, at, 1:2], hh[c, at, 2:3]
            else:
                pack = inputs[2 * other + at]
                x_links = pack[162 + c, 1:2], pack[162 + c, 4:5]
                t_links = pack[144 + c, 7:8], pack[144 + c, 2:3]
            vup[18 + c, y, BASE - 2 : BASE - 1] = x_links[0]
            vup[18 + c, y, BASE - 1 : BASE] = x_links[1]
            vdn[c, y, BASE + 8 : BASE + 9] = t_links[0]
            vdn[c, y, BASE + 9 : BASE + 10] = t_links[1]
        return 0

    lax.fori_loop(0, 18, corner, 0, unroll=2)

    for m in range(4):
        yy = ya[m] + 1

        def look(d, offset):
            source = {0: v0, 1: vup, -1: vdn}[offset[0]]
            row = BASE + 2 * offset[1]
            parts = [source[18 * d + c, yy + offset[2], row : row + 8] for c in range(18)]
            if offset[3] != 0:
                parts = [zroll(p, offset[3]) for p in parts]
            return as_matrix(parts)

        zero = (0, 0, 0, 0)
        others = [n for n in range(4) if n != m]
        for j, n in enumerate(others):
            step_m = tuple(int(k == m) for k in range(4))
            step_n = tuple(int(k == n) for k in range(4))
            back_n = tuple(-k for k in step_n)
            corner_mn = tuple(a - b for a, b in zip(step_m, step_n))
            up = mm(look(n, step_m), mm(look(n, zero), look(m, step_n)), b_dag=True)
            for c, value in enumerate(flat(up)):
                out[6 * m + 2 * j, c] = value
            down = mm(mm(look(m, back_n), look(n, corner_mn)), look(n, back_n), a_dag=True)
            for c, value in enumerate(flat(down)):
                out[6 * m + 2 * j + 1, c] = value


def even_rows():
    return lax.broadcasted_iota(jnp.int32, (8, 128), 0) % 2 == 0


def exchanged(a, b, even):
    return jnp.where(even, a, pltpu.roll(b, 1, 0)), jnp.where(even, pltpu.roll(a, 7, 0), b)


def unpack_kernel(x, own, *rows):
    even = even_rows()

    def body(i, _):
        own[i, 0], own[i, 1] = exchanged(x[i, 0:8], x[i, 8:16], even)
        if rows:
            for y in range(2):
                for t in range(2):
                    at = 8 * t + y
                    rows[0][i, y, t : t + 1] = x[i, at : at + 1]
                    rows[1][i, y, t : t + 1] = x[i, at + 6 : at + 7]
        return 0

    lax.fori_loop(0, 72, body, 0, unroll=8)


def tail_kernel(own, tail):
    def body(i, _):
        for y in range(2):
            tail[i, y] = own[i, y, 2:8]
        return 0

    lax.fori_loop(0, 72, body, 0, unroll=8)


def weights_kernel(conv_in, bias_in, conv_out, bias_out, *refs):
    outs, big, small = refs[:8], refs[8], refs[9]
    big[...] = jnp.zeros_like(big)
    small[...] = jnp.zeros_like(small)
    for layer in range(2):
        w_in, b_in, w_out, b_out = outs[4 * layer : 4 * layer + 4]
        for k in range(27):
            taps = [conv_in[layer, 3 * k + z].astype(F32) for z in range(3)]
            taps = jnp.concatenate(taps, axis=1)
            for half, planes in enumerate(HALVES[layer]):
                for a, plane in enumerate(planes):
                    at = 16 * k + 8 * half + 2 * a
                    big[at : at + 2, 0:192] = taps[2 * plane : 2 * plane + 2]
        w_in[...] = jnp.transpose(big[...])[0:192, 0:432].astype(BF16)
        small[0:64, 0:24] = conv_out[layer].astype(F32)
        w_out[...] = jnp.transpose(small[...])[0:24, 0:64].astype(BF16)
        small[:, 0:64] = jnp.broadcast_to(bias_in[layer : layer + 1], (128, 64))
        b_in[...] = jnp.transpose(small[...])[0:64]
        small[:, 0:24] = jnp.broadcast_to(bias_out[layer : layer + 1], (128, 24))
        b_out[...] = jnp.transpose(small[...])[0:24]


def last_kernel(ya, own, staples, f, f_s, w_in, b_in, w_out, b_out, out, packed, wts, sems):
    even = even_rows()

    def store(i, y, value, old):
        at_0 = y == 0
        tiles = jnp.where(at_0, value, old), jnp.where(at_0, old, value)
        packed[i, 0:8], packed[i, 8:16] = exchanged(*tiles, even)

    def copy(m):
        part = slice(18 * m, 18 * m + 18)
        return pltpu.make_async_copy(packed.at[part], out.at[part], sems.at[m])

    update(
        ya, own, staples, f, f_s, w_in, b_in, w_out, b_out, wts, store,
        done=lambda m: copy(m).start(),
    )
    for m in range(4):
        copy(m).wait()


def final_kernel(ya, own, staples, f, f_s, w_in, b_in, w_out, b_out, out, sent, wts):
    def store(i, y, value, old):
        out[i, y] = value
        out[i, 1 - y] = old

    update(ya, own, staples, f, f_s, w_in, b_in, w_out, b_out, wts, store, sent)


def update(
    ya, own, staples, f, f_s, w_in, b_in, w_out, b_out, wts, store, sent=None, done=None
):
    places = ((1, 1), (0, 0), (0, 1), (1, 0))
    sites = [(y, r // 2, r % 2) for y in range(2) for r in range(8)]
    columns = []
    for y, x, t in sites:
        tiles = []
        for a in range(3):
            for b in range(3):
                for c in range(3):
                    other, at = places[y + c]
                    tiles.append((f, f_s)[other][at, x + b, t + a])
        columns.append(jnp.concatenate(tiles, axis=0))
    g = jnp.dot(w_in[...], jnp.concatenate(columns, axis=1), preferred_element_type=F32)
    hidden = []
    for k in range(16):
        lanes = slice(128 * k, 128 * k + 128)
        part = zroll(g[0:64, lanes], -1) + g[64:128, lanes] + zroll(g[128:192, lanes], 1)
        hidden.append(jnp.tanh(part + b_in[...]).astype(BF16))
    weights = jnp.dot(w_out[...], jnp.concatenate(hidden, axis=1), preferred_element_type=F32)
    for k in range(16):
        row = 24 * (k % 8)
        wts[k // 8, row : row + 24] = weights[:, 128 * k : 128 * k + 128] + b_out[...]

    for m in range(4):
        y = ya[m]
        link = as_matrix([own[18 * m + c, y] for c in range(18)])
        total = None
        for k in range(6 * m, 6 * m + 6):
            w = wts[y, pl.ds(k, 8, stride=24), :]
            term = [w * staples[k, c] for c in range(18)]
            total = term if total is None else [a + b for a, b in zip(total, term)]
        are, aim = mm(link, as_matrix(total))
        trace_im = (aim[0][0] + aim[1][1] + aim[2][2]) * (1.0 / 3.0)
        low = []
        for i, k in ((0, 1), (0, 2), (1, 2)):
            low.append(-0.25 * (are[i][k] - are[k][i]))
            low.append(-0.25 * (aim[i][k] + aim[k][i]))
        low += [-0.5 * (aim[i][i] - trace_im) for i in range(3)]
        if sent is not None:
            for c in range(9):
                sent[9 * m + c] = low[c]
        for c, value in enumerate(rotated(low, link)):
            store(18 * m + c, y, value, own[18 * m + c, 1 - y])
        if done is not None:
            done(m)


def rotated(low, link):
    one = jnp.ones_like(low[0])
    full = [[None] * 3 for _ in range(3)]
    for i in range(3):
        full[i][i] = (one, low[6 + i])
    for at, (i, k) in enumerate(((0, 1), (0, 2), (1, 2))):
        re, im = low[2 * at], low[2 * at + 1]
        full[i][k] = (re, im)
        full[k][i] = (-re, im)
    adj_re, adj_im = [], []
    for i in range(3):
        row_re, row_im = [], []
        for j in range(3):
            first = cmul(full[(j + 1) % 3][(i + 1) % 3], full[(j + 2) % 3][(i + 2) % 3])
            second = cmul(full[(j + 1) % 3][(i + 2) % 3], full[(j + 2) % 3][(i + 1) % 3])
            row_re.append(first[0] - second[0])
            row_im.append(first[1] - second[1])
        adj_re.append(row_re)
        adj_im.append(row_im)
    det_re = det_im = None
    for k in range(3):
        product = cmul(full[0][k], (adj_re[k][0], adj_im[k][0]))
        det_re = product[0] if det_re is None else det_re + product[0]
        det_im = product[1] if det_im is None else det_im + product[1]
    twice = 2.0 / (det_re * det_re + det_im * det_im)
    scale_re = det_re * twice
    scale_im = -det_im * twice
    turned = flat(mm((adj_re, adj_im), link))
    current = flat(link)
    real, imag = [], []
    for c in range(9):
        re, im = cmul((turned[c], turned[9 + c]), (scale_re, scale_im))
        real.append(re - current[c])
        imag.append(im - current[9 + c])
    return real + imag


def shift_kernel(
    ya, own, right, tail, tp, far, far_tail, q_next, q_tp, q_far, own_o, pack_0, pack_1, ex
):
    for m in range(4):
        here = ya[m]
        there = 1 - here
        at = [18 * m + c for c in range(18)]

        def turn(q, links):
            return rotated([q[9 * m + c] for c in range(9)], as_matrix(links))

        def joined(one, more, y):
            return [jnp.concatenate([one[i, y], more[i, y]], axis=0) for i in at]

        at_0 = here == 0

        def by_y(i, if_here, if_there):
            return (
                (pack_0, jnp.where(at_0, if_here, if_there)),
                (pack_1, jnp.where(at_0, if_there, if_here)),
            )

        new, old = turn(q_next, joined(right, tail, there)), joined(right, tail, here)
        for c, i in enumerate(at):
            for y, (pack, rows) in enumerate(by_y(i, old[c], new[c])):
                block = jnp.concatenate([own[i, y, 4:8], rows[0:4]], axis=0)
                own_o[i, y] = block
                pack[i] = block
                pack[144 + i, 0:2] = own[i, y, 2:4]
                pack[144 + i, 2:4] = rows[4:6]
                ex[i, y, 0:2] = own[i, y, 4:6]
                ex[i, y, 2:4] = rows[6:8]
        new, old = turn(q_tp, [tp[i, there] for i in at]), [tp[i, here] for i in at]
        for c, i in enumerate(at):
            for y, (pack, rows) in enumerate(by_y(i, old[c], new[c])):
                pack[72 + i, 0:4] = rows[4:8]
                pack[144 + i, 4:6] = rows[2:4]
                ex[i, y, 4:6] = rows[4:6]
        new, old = turn(q_far, joined(far, far_tail, here)), joined(far, far_tail, there)
        for c, i in enumerate(at):
            for y, (pack, rows) in enumerate(by_y(i, new[c], old[c])):
                pack[72 + i, 4:8] = rows[0:4]
                pack[144 + i, 6:8] = rows[4:6]
                ex[i, y, 6:8] = rows[6:8]


VM = pl.BlockSpec(memory_space=pltpu.VMEM)
SM = pl.BlockSpec(memory_space=pltpu.SMEM)


def params(mib):
    return pltpu.CompilerParams(vmem_limit_bytes=mib * 1024 * 1024)


def run_weights(conv_in, bias_in, conv_out, bias_out):
    shapes = [((192, 432), BF16), ((64, 128), F32), ((24, 64), BF16), ((24, 128), F32)]
    return pl.pallas_call(
        weights_kernel,
        out_shape=[jax.ShapeDtypeStruct(*shape) for shape in shapes * 2],
        in_specs=[VM] * 4,
        out_specs=[VM] * 8,
        scratch_shapes=[pltpu.VMEM((512, 256), F32), pltpu.VMEM((128, 128), F32)],
        compiler_params=params(8),
        cost_estimate=pl.CostEstimate(flops=0, bytes_accessed=6_000_000, transcendentals=0),
        name="weights",
    )(conv_in, bias_in, conv_out, bias_out)


def run_unpack(x, rows):
    lengths = (8, 2, 2) if rows else (8,)
    return pl.pallas_call(
        unpack_kernel,
        out_shape=[jax.ShapeDtypeStruct((72, 2, n, 128), F32) for n in lengths],
        in_specs=[VM],
        out_specs=[VM] * len(lengths),
        compiler_params=params(8),
        cost_estimate=pl.CostEstimate(flops=0, bytes_accessed=2_000_000, transcendentals=0),
        name="unpack",
    )(x.reshape(72, 16, 128))


def run_tail(own):
    return pl.pallas_call(
        tail_kernel,
        out_shape=jax.ShapeDtypeStruct((72, 2, 6, 128), F32),
        in_specs=[VM],
        out_specs=VM,
        compiler_params=params(8),
        cost_estimate=pl.CostEstimate(flops=0, bytes_accessed=1_000_000, transcendentals=0),
        name="tail",
    )(own)


def run_traces(mode, half, ya, *inputs):
    rows = (16 if mode == "single" else 48 if mode == "wide" else 16)
    planes = HALVES[mode != "single"]
    planes = planes[0] + planes[1] if half == 2 else planes[half]
    channels = (8 * rows * (len(planes) // 3), 128)
    placed = [pltpu.VMEM((72, 2, 8, 128), F32)] if mode == "single" else []
    shape = ((rows, 16, 128), BF16) if half else (channels, F32)
    return pl.pallas_call(
        functools.partial(trace_kernel, mode, planes, half > 0),
        out_shape=jax.ShapeDtypeStruct(*shape),
        in_specs=[SM] + [VM] * len(inputs),
        out_specs=VM,
        scratch_shapes=([pltpu.VMEM(channels, F32)] if half else []) + placed,
        compiler_params=params(10),
        cost_estimate=pl.CostEstimate(flops=4_000_000, bytes_accessed=4_000_000, transcendentals=0),
        name="traces",
    )(ya, *inputs)


def run_staples(mode, ya, *inputs):
    return pl.pallas_call(
        functools.partial(staple_kernel, mode),
        out_shape=jax.ShapeDtypeStruct((24, 18, 8, 128), F32),
        in_specs=[SM] + [VM] * len(inputs),
        out_specs=VM,
        scratch_shapes=[pltpu.VMEM((72, 4, 24, 128), F32)] * 3,
        compiler_params=params(22),
        cost_estimate=pl.CostEstimate(
            flops=20_000_000, bytes_accessed=16_000_000, transcendentals=0
        ),
        name="staples",
    )(ya, *inputs)


def run_final(ya, own, staples, f, f_s, w_in, b_in, w_out, b_out, last):
    weights = [pltpu.VMEM((2, 192, 128), F32)]
    shapes = [(72, 16, 128)] if last else [(72, 2, 8, 128), (36, 8, 128)]
    return pl.pallas_call(
        last_kernel if last else final_kernel,
        out_shape=[jax.ShapeDtypeStruct(shape, F32) for shape in shapes],
        in_specs=[SM] + [VM] * 8,
        out_specs=[pl.BlockSpec(memory_space=pl.ANY) if last else VM] + [VM] * (len(shapes) - 1),
        scratch_shapes=(
            [pltpu.VMEM((72, 16, 128), F32)] + weights + [pltpu.SemaphoreType.DMA((4,))]
            if last
            else weights
        ),
        compiler_params=params(14),
        cost_estimate=pl.CostEstimate(flops=300_000_000, bytes_accessed=4_000_000, transcendentals=131072),
        name="rotate",
    )(ya, own, staples, f, f_s, w_in, b_in, w_out, b_out)


def run_shift(ya, *arrays):
    block, pack = (72, 2, 8, 128), (216, 8, 128)
    return pl.pallas_call(
        shift_kernel,
        out_shape=[jax.ShapeDtypeStruct(shape, F32) for shape in (block, pack, pack, block)],
        in_specs=[SM] + [VM] * 9,
        out_specs=[VM] * 4,
        compiler_params=params(12),
        cost_estimate=pl.CostEstimate(flops=8_000_000, bytes_accessed=6_000_000, transcendentals=0),
        name="shift",
    )(ya, *arrays)


def step(value, axis, by):
    count = lax.axis_size(axis)
    return lax.ppermute(value, axis, [((i + by) % count, i) for i in range(count)])


def diagonal(value, x_by, t_by):
    n_x, n_t = lax.axis_size("space"), lax.axis_size("tm")
    pairs = [
        ((i + x_by) % n_x * n_t + (k + t_by) % n_t, i * n_t + k)
        for i in range(n_x)
        for k in range(n_t)
    ]
    return lax.ppermute(value, ("space", "tm"), pairs)


def other_time(value, dim, x_by=0):
    if lax.axis_size("tm") == 2:
        return diagonal(value, x_by, 1)
    up = diagonal(lax.slice_in_dim(value, 0, 1, axis=dim), x_by, 1)
    down = diagonal(lax.slice_in_dim(value, 1, 2, axis=dim), x_by, -1)
    return jnp.concatenate([up, down], axis=dim)


def other_rows(value, x_by=0):
    split = value.reshape(value.shape[:-2] + (value.shape[-2] // 2, 2, 128))
    return other_time(split, split.ndim - 2, x_by).reshape(value.shape)


def active_rows(active_blocks):
    index = (lax.axis_index("tm"), lax.axis_index("space"), 2 * lax.axis_index("sub"))
    at = lax.dynamic_slice(active_blocks, (0, 0) + index, active_blocks.shape[:2] + (1, 1, 1))
    return jnp.where(at[:, :, 0, 0, 0] > 0, 0, 1).astype(jnp.int32)


def per_device(gauge_links, active_blocks, conv_in, bias_in, conv_out, bias_out):
    tp_raw = other_time(gauge_links, 2)
    own, first, last = run_unpack(gauge_links, True)
    ya = active_rows(active_blocks)
    weights = run_weights(conv_in, bias_in, conv_out, bias_out)

    right = step(first, "space", 1)
    left = step(last, "space", -1)
    tail = step(run_tail(own), "space", 1)
    own_s = step(own, "sub", 1)
    right, left, ya, weights = lax.optimization_barrier((right, left, ya, weights))
    ya = [ya[0], ya[1]]
    mixed = jnp.concatenate([left[18:36, :, 0:1], right[0:18, :, 1:2]], axis=2)
    co = other_time(mixed, 2)
    h = jnp.concatenate([left, right], axis=2)
    h_s = step(h, "sub", 1)
    (tp,) = run_unpack(tp_raw, False)
    tr = run_traces("single", 2, ya[0], own, own_s, tp, right).reshape(2, 4, 2, 16, 128)
    far = other_rows(right)
    full = other_traces(tr)
    full, co, far, tail = lax.optimization_barrier((full, co, far, tail))
    far_tail = other_rows(tail)
    tp_s, co_s = step(tp, "sub", 1), step(co, "sub", 1)
    f, staples = rim(
        full, lambda: run_staples("single", ya[0], own, own_s, tp, tp_s, h, h_s, co, co_s)
    )
    f_s = step(f, "sub", 1)
    own, q = run_final(ya[0], own, staples, f, f_s, *weights[:4], False)

    q_tp = other_rows(q)
    q_far = other_rows(q, 1)
    q_next = step(q, "space", 1)
    own, pack_0, pack_1, ex = run_shift(
        ya[0], own, right, tail, tp, far, far_tail, q_next, q_tp, q_far
    )

    other_0, other_1 = step(pack_0, "sub", 1), step(pack_1, "sub", 1)

    def staples_1():
        return run_staples("packs", ya[1], pack_0, pack_1, other_0, other_1)

    mode = "wide" if lax.axis_size("tm") == 2 else "packs"
    half = run_traces(mode, 0, ya[1], pack_0, pack_1, pack_0, ex)
    tr = run_traces(mode, 1, ya[1], half, pack_0, pack_1, other_0, ex)
    if mode == "wide":
        f = tr.reshape(2, 6, 4, 16, 128)
        staples = staples_1()
    else:
        f, staples = rim(other_traces(tr.reshape(2, 4, 2, 16, 128)), staples_1)
    f_s = step(f, "sub", 1)
    (out,) = run_final(ya[1], own, staples, f, f_s, *weights[4:], True)
    return out.reshape(4, 18, 2, 4, 2, 128)


def other_traces(tr):
    times = other_time(tr, 2)
    return jnp.concatenate([times[:, :, 1:2], tr, times[:, :, 0:1]], axis=2)


def rim(full, meanwhile):
    before = step(full[:, 3:4], "space", -1)
    after = step(full[:, 0:1], "space", 1)
    other = meanwhile()
    before, after, other = lax.optimization_barrier((before, after, other))
    return jnp.concatenate([before, full, after], axis=1), other


def solution(mesh):
    placed = (
        P(None, None, ("grp", "tm"), "space", "sub", None),
        P("grp", None, None, None, None),
        P(),
        P(),
        P(),
        P(),
    )
    return jax.shard_map(
        per_device,
        mesh=mesh,
        in_specs=placed,
        out_specs=P(None, None, ("grp", "tm"), "space", "sub", None),
        check_vma=False,
    )
```
